256 devices in a mesh: section: 8 (over y, z_hi), vocab: 32 (over x, z_lo, core).
Axes of the slice: x: 4, y: 4, z: 8 (z_hi: 2, z_lo: 4; z = z_hi * 4 + z_lo), core: 2. Of those that a mesh axis runs over, the one named last changes fastest.
Arguments:
- hidden: bfloat16 [256, 4608], P('vocab', 'section'), may hold values from -6 to 6
- table: bfloat16 [256000, 4608], P(('vocab', 'section')), may hold values from -0.25 to 0.25
- token_ids: int32 [256], P('vocab'), may hold values from 0 to 255999
- targets: int32 [256], P('vocab'), may hold values from 0 to 255999
- input_grad: bfloat16 [256, 4608], P('vocab', 'section'), may hold values from -0.119628906 to 0.119628906
- projection: bfloat16 [4608, 256], replicated, may hold values from -0.09375 to 0.09375
Outputs:
- token_loss: float32 [256], P('vocab')
- hidden_grad: bfloat16 [256, 4608], P('vocab', 'section')
- low_rank: float32 [256000, 256], P(('vocab', 'section'))
The draws below stay inside these ranges and needn't reach their ends.
All inputs are finite; a program needn't handle non-finite values.
Results may differ from the reference program's by a relative error of at most 0.0065.
Values may be sent and summed in bfloat16 or wider, within the bound.
A program may use at most 128 MiB of HBM per device.

```python
import math
import jax
import jax.numpy as jnp
import numpy as np
from jax import lax

D = 4608
V_DEV = 1000
RANK = 256
VOCAB = 256000
TOKENS = 256
N_SECTION = 8
N_VOCAB = 32


def place_ends(drawn, own_key, smallest, largest):
    spot = [jax.random.randint(jax.random.fold_in(own_key, axis), (), 0, length) for axis, length in enumerate(drawn.shape)]
    widest = drawn.shape.index(max(drawn.shape))
    next_to = spot[:widest] + [(spot[widest] + 1) % drawn.shape[widest]] + spot[widest + 1:]
    return drawn.at[tuple(spot)].set(smallest).at[tuple(next_to)].set(largest)


def steps_of(rng, shape, split, smallest, largest):
    def one(axis_at, blocks):
        steps = jax.random.uniform(jax.random.fold_in(jax.random.fold_in(rng, 6), axis_at), (blocks,), jnp.float32, smallest / len(split), largest / len(split))
        return jnp.repeat(jnp.exp(steps), shape[axis_at] // blocks).reshape((-1,) + (1,) * (len(shape) - axis_at - 1))

    loudness = one(*split[0])
    for cut in split[1:]:
        loudness = loudness * one(*cut)
    return loudness


def ranked_wide(stream_key, dims, number_of, skew):
    weights = [min(1 << octave, number_of + 1 - (1 << octave)) * (1 << 20) // math.isqrt((1 << octave) ** skew) + 1 for octave in range((number_of + 1).bit_length()) if 1 << octave <= number_of]
    spread = 1 + sum(weights) // (1 << 30)
    listing = np.cumsum(np.array([max(1, weight // spread) for weight in weights]))
    pick = jax.random.randint(jax.random.fold_in(stream_key, 1), dims, 0, int(listing[len(weights) - 1]))
    start = jnp.left_shift(1, jnp.searchsorted(jnp.asarray(listing, jnp.int32), pick, side="right").astype(jnp.int32))
    standing = start - 1 + jax.random.randint(jax.random.fold_in(stream_key, 4), dims, 0, 1 << 30) % jnp.minimum(start, number_of + 1 - start)
    return jax.random.permutation(jax.random.fold_in(stream_key, 2), number_of)[standing].astype(jnp.int32)


def scatter_about(rng, shape, spread, bound, split=(), kind=jnp.bfloat16):
    entries = jax.random.normal(rng, shape, jnp.float32) * spread
    if len(split) > 0:
        entries = steps_of(rng, shape, split, -0.22, 0.18) * entries
    return jnp.clip(entries, min=-bound, max=bound).astype(kind)


def setup_inputs(seed: int = 0) -> dict:
    splits = jax.random.split(jax.random.key(seed), 7)
    return {
        "hidden": scatter_about(splits[0], (TOKENS, D), 1.0, 6.0, ((0, 32), (1, 8))),
        "table": scatter_about(splits[1], (VOCAB, D), (D // 9) ** -0.5, 0.25, ((0, 256),)),
        "token_ids": place_ends(ranked_wide(splits[2], (TOKENS,), VOCAB, 2), jax.random.fold_in(splits[2], 3), 0, VOCAB - 1).astype(jnp.int32),
        "targets": place_ends(ranked_wide(splits[3], (TOKENS,), VOCAB, 2), jax.random.fold_in(splits[3], 3), 0, VOCAB - 1).astype(jnp.int32),
        "input_grad": scatter_about(splits[4], (TOKENS, D), 0.02, 0.119628906, ((0, 32), (1, 8))),
        "projection": scatter_about(splits[5], (D, RANK), D ** -0.5, 0.09375),
    }


def reference(hidden, table, token_ids, targets, input_grad, projection):
    blocks = N_VOCAB * N_SECTION
    stacked = table.reshape(blocks, V_DEV, D)
    starts = jnp.arange(blocks, dtype=jnp.int32) * V_DEV

    def logits_of(block):
        raw = lax.dot_general(hidden, block, (((1,), (1,)), ((), ())), preferred_element_type=jnp.float32)
        return 30.0 * jnp.tanh(raw / 30.0)

    def first_pass(pair):
        block, begin = pair
        capped = logits_of(block)
        columns = begin + jnp.arange(V_DEV, dtype=jnp.int32)
        hit = targets[:, None] == columns[None, :]
        return (lax.optimization_barrier(jnp.sum(jnp.exp(capped), axis=1)), lax.optimization_barrier(jnp.sum(jnp.where(hit, capped, 0.0), axis=1)))
    totals, picks = lax.map(first_pass, (stacked, starts))
    total = lax.optimization_barrier(jnp.sum(totals, axis=0))
    picked = lax.optimization_barrier(jnp.sum(picks, axis=0))
    token_loss = jnp.log(total) - picked
    hidden_proj = jnp.dot(hidden, projection, preferred_element_type=jnp.float32)
    input_proj = jnp.dot(input_grad, projection, preferred_element_type=jnp.float32)

    def second_pass(carry, pair):
        block, begin = pair
        capped = logits_of(block)
        columns = begin + jnp.arange(V_DEV, dtype=jnp.int32)
        hit = (targets[:, None] == columns[None, :]).astype(jnp.float32)
        dlogit = ((jnp.exp(capped) / total[:, None] - hit) * (1.0 - (capped / 30.0) ** 2)).astype(jnp.bfloat16)
        carry = carry + jnp.dot(dlogit, block, preferred_element_type=jnp.float32)
        head_part = lax.dot_general(dlogit.astype(jnp.float32), hidden_proj, (((0,), (0,)), ((), ())), precision=lax.Precision.HIGHEST)
        picks_ids = (token_ids[:, None] == columns[None, :]).astype(jnp.float32)
        embed_part = lax.dot_general(picks_ids, input_proj, (((0,), (0,)), ((), ())), precision=lax.Precision.HIGHEST)
        return (carry, head_part + math.sqrt(D) * embed_part)
    start_grad = jnp.zeros((TOKENS, D), jnp.float32)
    summed, pieces = lax.scan(second_pass, start_grad, (stacked, starts))
    return (token_loss, summed.astype(jnp.bfloat16), pieces.reshape(VOCAB, RANK))
```

```python
import math

import jax
import jax.numpy as jnp
from jax import lax
from jax.experimental import pallas as pl
from jax.experimental.pallas import tpu as pltpu
from jax.sharding import PartitionSpec as P

MESH = pl.DeviceIdType.MESH
F32 = jnp.float32
BF16 = jnp.bfloat16
NY = 4
NX = 4
NZ = 8
QUARTER = 1152
SECT = 576
PADDED = 640
ROWS = 1000
RANK = 256


def kernel(
    hidden_ref,
    table_hbm,
    ids_ref,
    targets_ref,
    input_ref,
    proj_hbm,
    loss_ref,
    grad_ref,
    low_ref,
    table,
    proj,
    zraw,
    zip_,
    hall,
    ipall,
    idbuf,
    arbuf,
    capped_s,
    expo_s,
    dmat,
    sib_out,
    sib_in,
    acc,
    w0,
    out1a,
    in1a,
    out1b,
    in1b,
    out2,
    in2,
    out3,
    in3,
    load_sem,
    zs,
    zr,
    ids_s,
    ids_r,
    ars,
    arr,
    ags,
    agr,
    css,
    csr,
    ips,
    ipr,
    ics,
    icr,
    xs,
    xr,
    r1s,
    r1r,
    r2s,
    r2r,
    r3s,
    r3r,
):
    sec = lax.axis_index("section")
    voc = lax.axis_index("vocab")
    y = sec // 2
    x = voc // 8
    z = (sec % 2) * 4 + (voc // 2) % 4
    c = voc % 2

    def dev(px, py, pz, pc):
        return {"section": py * 2 + pz // 4, "vocab": (px * 4 + pz % 4) * 2 + pc}

    zc = [
        dev(x, y, (z + dz) % NZ, (c + dc) % 2)
        for dc in range(2)
        for dz in range(NZ)
        if dz or dc
    ]
    xy = [
        dev((x + dx) % NX, (y + dy) % NY, z, c)
        for dx in range(NX)
        for dy in range(NY)
        if dx or dy
    ]
    sibling = dev(x, y, z, (c + 1) % 2)

    def send(src, dst, ssem, rsem, to):
        copy = pltpu.make_async_remote_copy(
            src_ref=src,
            dst_ref=dst,
            send_sem=ssem,
            recv_sem=rsem,
            device_id=to,
            device_id_type=MESH,
        )
        copy.start()
        return copy

    sent = []

    load_table = pltpu.make_async_copy(table_hbm, table, load_sem.at[0])
    load_table.start()
    load_proj = pltpu.make_async_copy(proj_hbm, proj, load_sem.at[1])
    load_proj.start()

    half, zz = (z % 4) // 2, z % 2
    base = half * 64 + x * 16 + zz * 8
    lane = lax.broadcasted_iota(jnp.int32, (1, 256), 1)
    tvec = jnp.zeros((1, 256), jnp.int32)
    ivec = jnp.zeros((1, 256), jnp.int32)
    for i in range(8):
        here = lane == base + i
        tvec = jnp.where(here, targets_ref[i], tvec)
        ivec = jnp.where(here, ids_ref[i], ivec)
    mine = sec == 0
    idbuf[0, :, 0:256] = jnp.where(mine, tvec, 0).astype(F32)
    idbuf[0, :, 256:512] = jnp.where(mine, ivec, 0).astype(F32)
    zraw[z, :, 0:SECT] = hidden_ref[...].astype(F32)

    barrier = pltpu.get_barrier_semaphore()
    for peer in zc + xy:
        pl.semaphore_signal(barrier, inc=1, device_id=peer, device_id_type=MESH)
    pl.semaphore_wait(barrier, len(zc) + len(xy))

    zcopies = [
        send(zraw.at[z], zraw.at[z], zs.at[dz - 1], zr.at[dz - 1], dev(x, y, (z + dz) % NZ, c))
        for dz in range(1, NZ)
    ]

    def swap(v):
        return jnp.concatenate(
            [v[:, 128:256], v[:, 0:128], v[:, 384:512], v[:, 256:384]], axis=1
        )

    def fold_zc(buf):
        same = jnp.sum(buf[0:8], axis=0)
        other = jnp.sum(buf[8:16], axis=0)
        return same + swap(other)

    id1 = [
        send(idbuf.at[0], idbuf.at[1 + i], ids_s.at[i], ids_r.at[i], p) for i, p in enumerate(zc)
    ]

    load_proj.wait()
    share = jnp.dot(
        input_ref[...], proj[pl.ds(pl.multiple_of(sec * SECT, 64), SECT), :], preferred_element_type=F32
    )
    zip_[z] = share

    for cp in zcopies:
        cp.wait_recv()
    for h in range(2):
        rows = []
        for k in range(2):
            zl = 2 * h + k
            rows.append(
                jnp.concatenate([zraw[zl][:, 0:SECT], zraw[zl + 4][:, 0:SECT]], axis=1)
            )
        hall[0, h, y, x] = jnp.concatenate(rows, axis=0).astype(BF16)

    stage2 = []
    for d in range(1, 4):
        px = dev((x + d) % NX, y, z, c)
        py = dev(x, (y + d) % NY, z, c)
        stage2.append(send(hall.at[0, 0, y, x], hall.at[0, 0, y, x], ags.at[d - 1], agr.at[d - 1], px))
        stage2.append(send(hall.at[0, 1, y, x], hall.at[0, 1, y, x], ags.at[d + 2], agr.at[d + 2], py))
    ipz = [
        send(zip_.at[z], zip_.at[z], ips.at[dz - 1], ipr.at[dz - 1], dev(x, y, (z + dz) % NZ, c))
        for dz in range(1, NZ)
    ]
    for cp in id1:
        cp.wait_recv()
    idbuf[16] = fold_zc(idbuf)
    id2 = [
        send(idbuf.at[16], idbuf.at[17 + i], ids_s.at[15 + i], ids_r.at[15 + i], p)
        for i, p in enumerate(xy)
    ]
    for cp in stage2:
        cp.wait_recv()
    stage3 = []
    for d in range(1, 4):
        px = dev((x + d) % NX, y, z, c)
        py = dev(x, (y + d) % NY, z, c)
        stage3.append(send(hall.at[0, 0, y], hall.at[0, 0, y], ags.at[d + 5], agr.at[d + 5], py))
        stage3.append(send(hall.at[0, 1, :, x], hall.at[0, 1, :, x], ags.at[d + 8], agr.at[d + 8], px))

    def to_sibling(k):
        fy, fx = (y + 4 - k) % 4, (x + 4 - k) % 4
        return [
            send(hall.at[0, 0, fy], hall.at[1, 0, fy], css.at[2 * k], csr.at[2 * k], sibling),
            send(hall.at[0, 1, :, fx], hall.at[1, 1, :, fx], css.at[2 * k + 1], csr.at[2 * k + 1], sibling),
        ]

    cross = to_sibling(0)
    for cp in ipz:
        cp.wait_recv()
    for h in range(2):
        block = jnp.concatenate(
            [zip_[2 * h] + zip_[2 * h + 4], zip_[2 * h + 1] + zip_[2 * h + 5]], axis=0
        )
        ipall[0, h, y, x] = block.astype(BF16)
    for cp in id2:
        cp.wait_recv()
    idvec = jnp.sum(idbuf[16:32], axis=0)
    targets = idvec[:, 0:256].astype(jnp.int32)
    ids = idvec[:, 256:512].astype(jnp.int32)

    for d in range(1, 4):
        stage3[2 * d - 2].wait_recv()
        stage3[2 * d - 1].wait_recv()
        cross += to_sibling(d)
    for cp in cross:
        cp.wait_recv()
    load_table.wait()

    ip2 = []
    for d in range(1, 4):
        px = dev((x + d) % NX, y, z, c)
        py = dev(x, (y + d) % NY, z, c)
        ip2.append(send(ipall.at[0, 0, y, x], ipall.at[0, 0, y, x], ips.at[d + 6], ipr.at[d + 6], px))
        ip2.append(send(ipall.at[0, 1, y, x], ipall.at[0, 1, y, x], ips.at[d + 9], ipr.at[d + 9], py))

    def tokens_of(ref, yy, width):
        return jnp.concatenate(
            [ref[p, h, yy].reshape(64, width) for p in range(2) for h in range(2)], axis=0
        )

    raw = jnp.zeros((ROWS, 256), F32)
    for yy in range(4):
        raw += lax.dot_general(
            table[:, yy * QUARTER : (yy + 1) * QUARTER],
            tokens_of(hall, yy, QUARTER),
            (((1,), (1,)), ((), ())),
            preferred_element_type=F32,
        )
    capped = 30.0 * jnp.tanh(raw / 30.0)
    expo = jnp.exp(capped)
    offset = (voc * 8 + sec) * ROWS
    row = offset + lax.broadcasted_iota(jnp.int32, (ROWS, 256), 0)
    hit = row == targets
    capped_s[...] = capped
    expo_s[...] = expo
    arbuf[0, :, 0:256] = jnp.sum(expo, axis=0, keepdims=True)
    arbuf[0, :, 256:512] = jnp.sum(jnp.where(hit, capped, 0.0), axis=0, keepdims=True)
    ar1 = [
        send(arbuf.at[0], arbuf.at[1 + i], ars.at[i], arr.at[i], p) for i, p in enumerate(zc)
    ]
    for cp in ip2:
        cp.wait_recv()
    ip3 = []
    for d in range(1, 4):
        px = dev((x + d) % NX, y, z, c)
        py = dev(x, (y + d) % NY, z, c)
        ip3.append(send(ipall.at[0, 0, y], ipall.at[0, 0, y], ips.at[d + 12], ipr.at[d + 12], py))
        ip3.append(send(ipall.at[0, 1, :, x], ipall.at[0, 1, :, x], ips.at[d + 15], ipr.at[d + 15], px))
    for cp in ar1:
        cp.wait_recv()
    arbuf[16] = fold_zc(arbuf)
    ar2 = [
        send(arbuf.at[16], arbuf.at[17 + i], ars.at[15 + i], arr.at[15 + i], p)
        for i, p in enumerate(xy)
    ]
    hproj = jnp.zeros((256, RANK), F32)
    for yy in range(4):
        hproj += jnp.dot(
            tokens_of(hall, yy, QUARTER),
            proj[yy * QUARTER : (yy + 1) * QUARTER, :],
            preferred_element_type=F32,
        )
    for cp in ar2:
        cp.wait_recv()
    sums = jnp.sum(arbuf[16:32], axis=0)
    total, picked = sums[:, 0:256], sums[:, 256:512]
    loss = jnp.log(total) - picked
    column = lax.broadcasted_iota(jnp.int32, (8, 256), 1)
    spot = base + lax.broadcasted_iota(jnp.int32, (8, 256), 0)
    loss_ref[...] = jnp.sum(jnp.where(column == spot, loss, 0.0), axis=1, keepdims=True)

    capped = capped_s[...]
    dlogit_t = (
        (expo_s[...] / total - (row == targets).astype(F32)) * (1.0 - (capped / 30.0) ** 2)
    ).astype(BF16)
    dmat[...] = dlogit_t.T

    cross_out = []
    for k in range(4):
        yy = (y + (2, 1, 3, 0)[k]) % 4
        part = jnp.dot(
            dmat[...],
            table[:, pl.ds(pl.multiple_of(yy * QUARTER, 128), QUARTER)],
            preferred_element_type=F32,
        )
        sib_out[k] = part[128:256].astype(BF16).reshape(2, 4, 16, QUARTER)
        cross_out.append(send(sib_out.at[k], sib_in.at[k], xs.at[k], xr.at[k], sibling))
        acc[k] = part[0:128].reshape(2, 4, 16, QUARTER)
    first = []
    for k in range(4):
        dy = (2, 1, 3, 0)[k]
        cross_out[k].wait_recv()
        acc[k] = acc[k] + sib_in[k].astype(F32)
        if dy:
            out1a[k] = acc[k, 0].astype(BF16)
            first.append(send(out1a.at[k], in1a.at[k], r1s.at[k], r1r.at[k], dev(x, (y + dy) % NY, z, c)))
        for d in range(1, 4):
            xx = (x + d) % NX
            out1b[k, d - 1] = acc[k, 1, xx].astype(BF16)
            slot = 2 + 3 * k + d
            first.append(
                send(out1b.at[k, d - 1], in1b.at[k, d - 1], r1s.at[slot], r1r.at[slot], dev(xx, y, z, c))
            )

    for cp in ip3:
        cp.wait_recv()
    icross = []
    for k in range(4):
        fy = (y + 4 - k) % 4
        icross.append(send(ipall.at[0, 0, fy], ipall.at[1, 0, fy], ics.at[2 * k], icr.at[2 * k], sibling))
        fx = (x + 4 - k) % 4
        icross.append(
            send(ipall.at[0, 1, :, fx], ipall.at[1, 1, :, fx], ics.at[2 * k + 1], icr.at[2 * k + 1], sibling)
        )

    for cp in first:
        cp.wait_recv()
    w0[...] = acc[3, 0]
    for k in range(3):
        w0[...] = w0[...] + in1a[k].astype(F32)
    second = []
    for d in range(1, 4):
        xx = (x + d) % NX
        out2[0, d - 1] = w0[xx].astype(BF16)
        second.append(send(out2.at[0, d - 1], in2.at[0, d - 1], r2s.at[d - 1], r2r.at[d - 1], dev(xx, y, z, c)))
    for k in range(4):
        w1 = acc[k, 1, x]
        for d in range(3):
            w1 = w1 + in1b[k, d].astype(F32)
        if k < 3:
            dy = (2, 1, 3)[k]
            out2[1, k] = w1.astype(BF16)
            second.append(
                send(out2.at[1, k], in2.at[1, k], r2s.at[3 + k], r2r.at[3 + k], dev(x, (y + dy) % NY, z, c))
            )

    def split(v):
        upper = v.astype(BF16)
        return upper, (v - upper.astype(F32)).astype(BF16)

    for cp in icross:
        cp.wait_recv()
    hp_hi, hp_lo = split(hproj)
    iproj = tokens_of(ipall, 0, RANK).astype(F32)
    for yy in range(1, 4):
        iproj = iproj + tokens_of(ipall, yy, RANK).astype(F32)
    ip_hi, ip_lo = split(iproj * math.sqrt(NY * QUARTER))
    picks = (row == ids).astype(BF16)
    low_ref[...] = (
        jnp.dot(dlogit_t, hp_hi, preferred_element_type=F32)
        + jnp.dot(dlogit_t, hp_lo, preferred_element_type=F32)
        + jnp.dot(picks, ip_hi, preferred_element_type=F32)
        + jnp.dot(picks, ip_lo, preferred_element_type=F32)
    )

    for cp in second:
        cp.wait_recv()
    halves = []
    own0 = w0[x]
    for d in range(3):
        own0 = own0 + in2[0, d].astype(F32)
        w1 = w1 + in2[1, d].astype(F32)
    halves = (own0, w1)
    for zl in range(4):
        block = halves[zl // 2][8 * (zl % 2) : 8 * (zl % 2) + 8]
        out3[zl, :, 0:SECT] = block[:, 0:SECT]
        out3[zl + 4, :, 0:SECT] = block[:, SECT:QUARTER]
    third = [
        send(out3.at[(z + dz) % NZ], in3.at[z], r3s.at[dz - 1], r3r.at[dz - 1], dev(x, y, (z + dz) % NZ, c))
        for dz in range(1, NZ)
    ]
    in3[z] = out3[z]
    for cp in third:
        cp.wait_recv()
    grad = in3[0]
    for k in range(1, NZ):
        grad = grad + in3[k]
    grad_ref[...] = grad[:, 0:SECT].astype(BF16)
    for group in (
        zcopies, id1, stage2, ipz, id2, stage3, cross, ip2, ar1, ip3, ar2, cross_out, first, icross, second, third
    ):
        for cp in group:
            cp.wait_send()


def per_device(hidden, table, token_ids, targets, input_grad, projection):
    dma = pltpu.SemaphoreType.DMA
    vmem = pl.BlockSpec(memory_space=pltpu.VMEM)
    smem = pl.BlockSpec(memory_space=pltpu.SMEM)
    hbm = pl.BlockSpec(memory_space=pl.ANY)
    loss, grad, low = pl.pallas_call(
        kernel,
        out_shape=(
            jax.ShapeDtypeStruct((8, 1), F32),
            jax.ShapeDtypeStruct((8, SECT), BF16),
            jax.ShapeDtypeStruct((ROWS, RANK), F32),
        ),
        in_specs=[vmem, hbm, smem, smem, vmem, hbm],
        out_specs=(vmem, vmem, vmem),
        scratch_shapes=[
            pltpu.VMEM((ROWS, NY * QUARTER), BF16),
            pltpu.VMEM((NY * QUARTER, RANK), BF16),
            pltpu.VMEM((NZ, 8, PADDED), F32),
            pltpu.VMEM((NZ, 8, RANK), F32),
            pltpu.VMEM((2, 2, NY, NX, 16, QUARTER), BF16),
            pltpu.VMEM((2, 2, NY, NX, 16, RANK), BF16),
            pltpu.VMEM((32, 1, 512), F32),
            pltpu.VMEM((32, 1, 512), F32),
            pltpu.VMEM((ROWS, 256), F32),
            pltpu.VMEM((ROWS, 256), F32),
            pltpu.VMEM((256, ROWS), BF16),
            pltpu.VMEM((4, 2, NX, 16, QUARTER), BF16),
            pltpu.VMEM((4, 2, NX, 16, QUARTER), BF16),
            pltpu.VMEM((4, 2, NX, 16, QUARTER), F32),
            pltpu.VMEM((NX, 16, QUARTER), F32),
            pltpu.VMEM((3, NX, 16, QUARTER), BF16),
            pltpu.VMEM((3, NX, 16, QUARTER), BF16),
            pltpu.VMEM((4, 3, 16, QUARTER), BF16),
            pltpu.VMEM((4, 3, 16, QUARTER), BF16),
            pltpu.VMEM((2, 3, 16, QUARTER), BF16),
            pltpu.VMEM((2, 3, 16, QUARTER), BF16),
            pltpu.VMEM((NZ, 8, PADDED), F32),
            pltpu.VMEM((NZ, 8, PADDED), F32),
            dma((2,)),
            dma((7,)), dma((7,)),
            dma((30,)), dma((30,)),
            dma((30,)), dma((30,)),
            dma((12,)), dma((12,)),
            dma((8,)), dma((8,)),
            dma((19,)), dma((19,)),
            dma((8,)), dma((8,)),
            dma((4,)), dma((4,)),
            dma((15,)), dma((15,)),
            dma((6,)), dma((6,)),
            dma((7,)), dma((7,)),
        ],
        compiler_params=pltpu.CompilerParams(
            collective_id=0, has_side_effects=True, vmem_limit_bytes=58 * 2**20
        ),
        cost_estimate=pl.CostEstimate(flops=6 * 10**9, bytes_accessed=13 * 10**6, transcendentals=512000),
    )(hidden, table, token_ids, targets, input_grad, projection)
    return loss.reshape(8), grad, low


def solution(mesh):
    placed = (
        P("vocab", "section"),
        P(("vocab", "section"), None),
        P("vocab"),
        P("vocab"),
        P("vocab", "section"),
        P(),
    )
    return jax.shard_map(
        per_device,
        mesh=mesh,
        in_specs=placed,
        out_specs=(P("vocab"), P("vocab", "section"), P(("vocab", "section"), None)),
        check_vma=False,
    )
```

```python
import math

import jax
import jax.numpy as jnp
from jax import lax
from jax.experimental import pallas as pl
from jax.experimental.pallas import tpu as pltpu
from jax.sharding import PartitionSpec as P

MESH = pl.DeviceIdType.MESH
F32 = jnp.float32
BF16 = jnp.bfloat16
NY = 4
NX = 4
NZ = 8
QUARTER = 1152
SECT = 576
PIECE = 288
ROWS = 1000
RANK = 256
FAR = (2, 1, 3, 0)


def kernel(
    hidden_ref,
    table_hbm,
    ids_ref,
    targets_ref,
    input_ref,
    proj_hbm,
    loss_ref,
    grad_ref,
    low_ref,
    table,
    proj,
    zraw,
    ipz,
    hall,
    ipy,
    ipx,
    idbuf,
    arbuf,
    capped_s,
    expo_s,
    dmat,
    scale,
    sib_out,
    sib_in,
    acc,
    tsib_out,
    tsib_in,
    tacc,
    tin0,
    tin1,
    out1a,
    in1a,
    out1b,
    in1b,
    out2,
    in2,
    out3,
    in3,
    load_sem,
    zs,
    zr,
    ids_s,
    ids_r,
    ars,
    arr,
    ags,
    agr,
    css,
    csr,
    ips,
    ipr,
    xs,
    xr,
    txs,
    txr,
    ts,
    tr,
    r1s,
    r1r,
    r2s,
    r2r,
    r3s,
    r3r,
):
    sec = lax.axis_index("section")
    voc = lax.axis_index("vocab")
    y = sec // 2
    x = voc // 8
    z = (sec % 2) * 4 + (voc // 2) % 4
    c = voc % 2

    def dev(px, py, pz, pc):
        return {"section": py * 2 + pz // 4, "vocab": (px * 4 + pz % 4) * 2 + pc}

    zc = [
        dev(x, y, (z + dz) % NZ, (c + dc) % 2)
        for dc in range(2)
        for dz in range(NZ)
        if dz or dc
    ]
    xy = [
        dev((x + dx) % NX, (y + dy) % NY, z, c)
        for dx in range(NX)
        for dy in range(NY)
        if dx or dy
    ]
    sibling = dev(x, y, z, (c + 1) % 2)

    def xpeer(d):
        return dev((x + d) % NX, y, z, c)

    def ypeer(d):
        return dev(x, (y + d) % NY, z, c)

    def zpeer(d):
        return dev(x, y, (z + d) % NZ, c)

    started = []

    def send(src, dst, sems, slot, to):
        copy = pltpu.make_async_remote_copy(
            src_ref=src,
            dst_ref=dst,
            send_sem=sems[0].at[slot],
            recv_sem=sems[1].at[slot],
            device_id=to,
            device_id_type=MESH,
        )
        copy.start()
        started.append(copy)
        return copy

    def arrive(copies):
        for copy in copies:
            copy.wait_recv()

    load_table = pltpu.make_async_copy(table_hbm, table, load_sem.at[0])
    load_table.start()
    load_proj = pltpu.make_async_copy(proj_hbm, proj, load_sem.at[1])
    load_proj.start()

    half, zz = (z % 4) // 2, z % 2
    base = half * 64 + x * 16 + zz * 8
    lane = lax.broadcasted_iota(jnp.int32, (1, 256), 1)
    tvec = jnp.zeros((1, 256), jnp.int32)
    ivec = jnp.zeros((1, 256), jnp.int32)
    for i in range(8):
        here = lane == base + i
        tvec = jnp.where(here, targets_ref[i], tvec)
        ivec = jnp.where(here, ids_ref[i], ivec)
    mine = sec == 0
    idbuf[0, :, 0:256] = jnp.where(mine, tvec, 0).astype(F32)
    idbuf[0, :, 256:512] = jnp.where(mine, ivec, 0).astype(F32)

    def pack(v):
        return jnp.concatenate([v[:, 0:PIECE], v[:, PIECE:SECT]], axis=0)

    def unpack(v):
        return jnp.concatenate([v[0:8, 0:PIECE], v[8:16, 0:PIECE]], axis=1)

    zraw[z, :, 0:PIECE] = pack(hidden_ref[...].astype(F32)).astype(BF16)

    barrier = pltpu.get_barrier_semaphore()
    for peer in zc + xy:
        pl.semaphore_signal(barrier, inc=1, device_id=peer, device_id_type=MESH)
    pl.semaphore_wait(barrier, len(zc) + len(xy))

    zcopies = [send(zraw.at[z], zraw.at[z], (zs, zr), d - 1, zpeer(d)) for d in range(1, NZ)]

    def swap(v):
        return jnp.concatenate(
            [v[:, 128:256], v[:, 0:128], v[:, 384:512], v[:, 256:384]], axis=1
        )

    def sum_zc(buf):
        return jnp.sum(buf[0:8], axis=0) + swap(jnp.sum(buf[8:16], axis=0))

    id1 = [send(idbuf.at[0], idbuf.at[1 + i], (ids_s, ids_r), i, p) for i, p in enumerate(zc)]

    load_proj.wait()
    ipz[z] = jnp.dot(
        input_ref[...],
        proj[pl.ds(pl.multiple_of(sec * SECT, 64), SECT), :],
        preferred_element_type=F32,
    )

    arrive(zcopies)
    for h in range(2):
        rows = []
        for k in range(2):
            zl = 2 * h + k
            low_part = unpack(zraw[zl].astype(F32))
            high_part = unpack(zraw[zl + 4].astype(F32))
            rows.append(jnp.concatenate([low_part, high_part], axis=1))
        hall[0, h, y, x] = jnp.concatenate(rows, axis=0).astype(BF16)

    ag = (ags, agr)
    near = {}
    far = {}

    def spread(j):
        bx, by = (x + 4 - j) % NX, (y + 4 - j) % NY
        for d in (1, 3, 2):
            far[0, j, d] = send(hall.at[0, 0, y, bx], hall.at[0, 0, y, bx], ag, 6 + 3 * j + d - 1, ypeer(d))
            far[1, j, d] = send(hall.at[0, 1, by, x], hall.at[0, 1, by, x], ag, 18 + 3 * j + d - 1, xpeer(d))

    for d in (1, 3, 2):
        near[0, d] = send(hall.at[0, 0, y, x], hall.at[0, 0, y, x], ag, d - 1, xpeer(d))
        near[1, d] = send(hall.at[0, 1, y, x], hall.at[0, 1, y, x], ag, 2 + d, ypeer(d))
    spread(0)
    ip = (ips, ipr)
    ipzc = [send(ipz.at[z], ipz.at[z], ip, d - 1, zpeer(d)) for d in range(1, NZ)]
    arrive(id1)
    idbuf[16] = sum_zc(idbuf)
    for j in (1, 3, 2):
        arrive([near[0, j], near[1, j]])
        spread(j)
    id2 = [
        send(idbuf.at[16], idbuf.at[17 + i], (ids_s, ids_r), 15 + i, p) for i, p in enumerate(xy)
    ]
    arrive(ipzc)
    for h in range(2):
        ipy[y, h] = jnp.concatenate(
            [ipz[2 * h] + ipz[2 * h + 4], ipz[2 * h + 1] + ipz[2 * h + 5]], axis=0
        ).astype(BF16)
    ipyc = [send(ipy.at[y], ipy.at[y], ip, 6 + d, ypeer(d)) for d in range(1, 4)]
    load_table.wait()
    arrive(id2)
    idvec = jnp.sum(idbuf[16:32], axis=0)
    targets = idvec[:, 0:256].astype(jnp.int32)
    ids = idvec[:, 256:512].astype(jnp.int32)
    offset = (voc * 8 + sec) * ROWS
    row = offset + lax.broadcasted_iota(jnp.int32, (ROWS, 256), 0)

    dmat[...] = (row == targets).astype(F32).astype(BF16).T
    tcross = []
    for k in range(4):
        yy = (y + FAR[k]) % NY
        part = jnp.dot(
            dmat[...],
            table[:, pl.ds(pl.multiple_of(yy * QUARTER, 128), QUARTER)],
            preferred_element_type=F32,
        ).astype(BF16)
        tsib_out[k] = part[128:256].reshape(2, NX, 16, QUARTER)
        tcross.append(send(tsib_out.at[k], tsib_in.at[k], (txs, txr), k, sibling))
        tacc[k] = part[0:128].reshape(2, NX, 16, QUARTER)

    cross = []
    for j in (0, 1, 3, 2):
        bx, by = (x + 4 - j) % NX, (y + 4 - j) % NY
        arrive([far[h, j, d] for h in range(2) for d in range(1, 4)])
        cross.append(send(hall.at[0, 0, :, bx], hall.at[1, 0, :, bx], (css, csr), 2 * j, sibling))
        cross.append(send(hall.at[0, 1, by], hall.at[1, 1, by], (css, csr), 2 * j + 1, sibling))

    for k in range(4):
        arrive([tcross[k]])
        tacc[k] = tacc[k] + tsib_in[k]
    tfirst = []
    for k in range(3):
        tfirst.append(send(tacc.at[k, 0], tin0.at[k], (ts, tr), k, ypeer(FAR[k])))
        xx = (x + FAR[k]) % NX
        tfirst.append(send(tacc.at[:, 1, xx], tin1.at[k], (ts, tr), 3 + k, xpeer(FAR[k])))
    arrive(cross)

    def tokens_of(yy):
        return jnp.concatenate(
            [hall[p, h, yy].reshape(64, QUARTER) for p in range(2) for h in range(2)], axis=0
        )

    raw = jnp.zeros((ROWS, 256), F32)
    for yy in range(4):
        raw += lax.dot_general(
            table[:, yy * QUARTER : (yy + 1) * QUARTER],
            tokens_of(yy),
            (((1,), (1,)), ((), ())),
            preferred_element_type=F32,
        )
    capped = 30.0 * jnp.tanh(raw / 30.0)
    expo = jnp.exp(capped)
    hit = row == targets
    capped_s[...] = capped
    expo_s[...] = expo
    arbuf[0, :, 0:256] = jnp.sum(expo, axis=0, keepdims=True)
    arbuf[0, :, 256:512] = jnp.sum(jnp.where(hit, capped, 0.0), axis=0, keepdims=True)
    ar1 = [send(arbuf.at[0], arbuf.at[1 + i], (ars, arr), i, p) for i, p in enumerate(zc)]

    dmat[...] = jnp.where(hit, 0.0, expo * (1.0 - (capped / 30.0) ** 2)).astype(BF16).T
    r1 = (r1s, r1r)
    first0 = {}
    first1 = {}
    crossed = []

    def first_sends(k):
        arrive([crossed[k]])
        acc[k] = acc[k] + sib_in[k].astype(F32)
        for j in range(3):
            dx = FAR[j]
            xx = (x + dx) % NX
            out1b[k, j] = acc[k, 1, xx].astype(BF16)
            first1[k, j] = send(out1b.at[k, j], in1b.at[k, j], r1, 12 + 3 * k + j, xpeer(dx))
            if k < 3:
                out1a[k, j] = acc[k, 0, xx].astype(BF16)
                first0[k, j] = send(out1a.at[k, j], in1a.at[k, j], r1, 4 * k + j, ypeer(FAR[k]))

    for k in range(4):
        yy = (y + FAR[k]) % NY
        part = jnp.dot(
            dmat[...],
            table[:, pl.ds(pl.multiple_of(yy * QUARTER, 128), QUARTER)],
            preferred_element_type=F32,
        )
        sib_out[k] = part[128:256].astype(BF16).reshape(2, NX, 16, QUARTER)
        crossed.append(send(sib_out.at[k], sib_in.at[k], (xs, xr), k, sibling))
        acc[k] = part[0:128].reshape(2, NX, 16, QUARTER)
        if k:
            first_sends(k - 1)
    first_sends(3)
    for k in range(3):
        out1a[k, 3] = acc[k, 0, x].astype(BF16)
        first0[k, 3] = send(out1a.at[k, 3], in1a.at[k, 3], r1, 4 * k + 3, ypeer(FAR[k]))

    arrive(ar1)
    arbuf[16] = sum_zc(arbuf)
    ar2 = [send(arbuf.at[16], arbuf.at[17 + i], (ars, arr), 15 + i, p) for i, p in enumerate(xy)]
    arrive(ipyc)
    ipx[0, x] = (
        ipy[0].astype(F32) + ipy[1].astype(F32) + ipy[2].astype(F32) + ipy[3].astype(F32)
    ).astype(BF16)
    ipxc = [send(ipx.at[0, x], ipx.at[0, x], ip, 9 + d, xpeer(d)) for d in range(1, 4)]
    hproj = jnp.zeros((256, RANK), F32)
    for yy in range(4):
        hproj += jnp.dot(
            tokens_of(yy), proj[yy * QUARTER : (yy + 1) * QUARTER, :], preferred_element_type=F32
        )
    arrive(ar2)
    sums = jnp.sum(arbuf[16:32], axis=0)
    total, picked = sums[:, 0:256], sums[:, 256:512]
    inverse = 1.0 / total
    target_coef = (jnp.exp(picked) / total - 1.0) * (1.0 - (picked / 30.0) ** 2)
    scale[0] = jnp.broadcast_to(inverse[:, 0:128], (128, 128)).T.reshape(2, NX, 16, 128)
    scale[1] = jnp.broadcast_to(target_coef[:, 0:128], (128, 128)).T.reshape(2, NX, 16, 128)

    def scaled(u, t, h, xx):
        return u * scale[0, h, xx][:, 0:1] + t * scale[1, h, xx][:, 0:1]

    arrive(tfirst)
    r2 = (r2s, r2r)
    second = []
    kept = {}

    def step0(j):
        arrive([first0[k, j] for k in range(3)])
        xx = (x + FAR[j]) % NX
        u = acc[3, 0, xx]
        t = tacc[3, 0, xx].astype(F32)
        for k in range(3):
            u = u + in1a[k, j].astype(F32)
            t = t + tin0[k, xx].astype(F32)
        s = scaled(u, t, 0, xx)
        if j < 3:
            out2[0, j] = s.astype(BF16)
            second.append(send(out2.at[0, j], in2.at[0, j], r2, j, xpeer(FAR[j])))
        else:
            kept[0] = s

    def step1(k):
        arrive([first1[k, j] for j in range(3)])
        u = acc[k, 1, x]
        t = tacc[k, 1, x].astype(F32)
        for j in range(3):
            u = u + in1b[k, j].astype(F32)
            t = t + tin1[j, k].astype(F32)
        s = scaled(u, t, 1, x)
        if k < 3:
            out2[1, k] = s.astype(BF16)
            second.append(send(out2.at[1, k], in2.at[1, k], r2, 3 + k, ypeer(FAR[k])))
        else:
            kept[1] = s

    step1(0)
    step1(1)
    step0(0)
    step1(2)
    step0(1)
    step0(2)
    step1(3)
    step0(3)
    arrive(ipxc)
    ipcross = send(ipx.at[0], ipx.at[1], ip, 13, sibling)

    arrive(second)
    for zl in range(4):
        h = zl // 2
        if zl % 2 == 0:
            whole = kept[h]
            for j in range(3):
                whole = whole + in2[h, j].astype(F32)
        block = whole[8 * (zl % 2) : 8 * (zl % 2) + 8]
        out3[zl, :, 0:PIECE] = pack(block[:, 0:SECT]).astype(BF16)
        out3[zl + 4, :, 0:PIECE] = pack(block[:, SECT:QUARTER]).astype(BF16)
    third = [
        send(out3.at[(z + d) % NZ], in3.at[z], (r3s, r3r), d - 1, zpeer(d)) for d in range(1, NZ)
    ]
    in3[z] = out3[z]

    loss = jnp.log(total) - picked
    for i in range(8):
        loss_ref[i] = jnp.sum(jnp.where(lane == base + i, loss, 0.0))

    def split(v):
        upper = v.astype(BF16)
        return upper, (v - upper.astype(F32)).astype(BF16)

    dlogit_t = (
        (expo_s[...] / total - (row == targets).astype(F32)) * (1.0 - (capped_s[...] / 30.0) ** 2)
    ).astype(BF16)
    arrive([ipcross])
    iproj = jnp.concatenate(
        [
            jnp.concatenate([ipx[p, xx, h] for xx in range(NX)], axis=0)
            for p in range(2)
            for h in range(2)
        ],
        axis=0,
    ).astype(F32)
    hp_hi, hp_lo = split(hproj)
    ip_hi, ip_lo = split(iproj * math.sqrt(NY * QUARTER))
    picks = (row == ids).astype(F32).astype(BF16)
    low_ref[...] = (
        jnp.dot(dlogit_t, hp_hi, preferred_element_type=F32)
        + jnp.dot(dlogit_t, hp_lo, preferred_element_type=F32)
        + jnp.dot(picks, ip_hi, preferred_element_type=F32)
        + jnp.dot(picks, ip_lo, preferred_element_type=F32)
    )

    arrive(third)
    grad = in3[0].astype(F32)
    for k in range(1, NZ):
        grad = grad + in3[k].astype(F32)
    grad_ref[...] = unpack(grad).astype(BF16)
    for copy in started:
        copy.wait_send()


def hand_over(loss_in, grad_in, low_in, loss_out, grad_out, low_out):
    low_out[...] = low_in[...]
    grad_out[...] = grad_in[...]
    for i in range(8):
        loss_out[i] = loss_in[i]


def per_device(hidden, table, token_ids, targets, input_grad, projection):
    dma = pltpu.SemaphoreType.DMA
    vmem = pl.BlockSpec(memory_space=pltpu.VMEM)
    smem = pl.BlockSpec(memory_space=pltpu.SMEM)
    hbm = pl.BlockSpec(memory_space=pl.ANY)
    shapes = (
        jax.ShapeDtypeStruct((8,), F32),
        jax.ShapeDtypeStruct((8, SECT), BF16),
        jax.ShapeDtypeStruct((ROWS, RANK), F32),
    )

    def blocks(n, kind=BF16):
        return pltpu.VMEM((n, 2, NX, 16, QUARTER), kind)

    def pairs(*counts):
        return [dma((n,)) for n in counts for _ in range(2)]

    outs = pl.pallas_call(
        kernel,
        out_shape=shapes,
        in_specs=[vmem, hbm, smem, smem, vmem, hbm],
        out_specs=(smem, vmem, vmem),
        scratch_shapes=[
            pltpu.VMEM((ROWS, NY * QUARTER), BF16),
            pltpu.VMEM((NY * QUARTER, RANK), BF16),
            pltpu.VMEM((NZ, 16, 384), BF16),
            pltpu.VMEM((NZ, 8, RANK), F32),
            pltpu.VMEM((2, 2, NY, NX, 16, QUARTER), BF16),
            pltpu.VMEM((NY, 2, 16, RANK), BF16),
            pltpu.VMEM((2, NX, 2, 16, RANK), BF16),
            pltpu.VMEM((32, 1, 512), F32),
            pltpu.VMEM((32, 1, 512), F32),
            pltpu.VMEM((ROWS, 256), F32),
            pltpu.VMEM((ROWS, 256), F32),
            pltpu.VMEM((256, ROWS), BF16),
            pltpu.VMEM((2, 2, NX, 16, 128), F32),
            blocks(4),
            blocks(4),
            blocks(4, F32),
            blocks(4),
            blocks(4),
            blocks(4),
            pltpu.VMEM((3, NX, 16, QUARTER), BF16),
            pltpu.VMEM((3, 4, 16, QUARTER), BF16),
            pltpu.VMEM((3, 4, 16, QUARTER), BF16),
            pltpu.VMEM((3, 4, 16, QUARTER), BF16),
            pltpu.VMEM((4, 3, 16, QUARTER), BF16),
            pltpu.VMEM((4, 3, 16, QUARTER), BF16),
            pltpu.VMEM((2, 3, 16, QUARTER), BF16),
            pltpu.VMEM((2, 3, 16, QUARTER), BF16),
            pltpu.VMEM((NZ, 16, 384), BF16),
            pltpu.VMEM((NZ, 16, 384), BF16),
            dma((2,)),
            *pairs(7, 30, 30, 30, 8, 14, 4, 4, 6, 24, 6, 7),
        ],
        compiler_params=pltpu.CompilerParams(
            collective_id=0, has_side_effects=True, vmem_limit_bytes=58 * 2**20
        ),
        cost_estimate=pl.CostEstimate(
            flops=8 * 10**9, bytes_accessed=13 * 10**6, transcendentals=512000
        ),
    )(hidden, table, token_ids, targets, input_grad, projection)
    return pl.pallas_call(
        hand_over,
        out_shape=shapes,
        in_specs=[smem, vmem, vmem],
        out_specs=(smem, vmem, vmem),
    )(*outs)


def solution(mesh):
    placed = (
        P("vocab", "section"),
        P(("vocab", "section"), None),
        P("vocab"),
        P("vocab"),
        P("vocab", "section"),
        P(),
    )
    return jax.shard_map(
        per_device,
        mesh=mesh,
        in_specs=placed,
        out_specs=(P("vocab"), P("vocab", "section"), P(("vocab", "section"), None)),
        check_vma=False,
    )
```

```python
import math

import jax
import jax.numpy as jnp
from jax import lax
from jax.experimental import pallas as pl
from jax.experimental.pallas import tpu as pltpu
from jax.sharding import PartitionSpec as P

MESH = pl.DeviceIdType.MESH
F32 = jnp.float32
BF16 = jnp.bfloat16
NY = 4
NX = 4
NZ = 8
QUARTER = 1152
SECT = 576
PIECE = 288
ROWS = 1000
RANK = 256
FAR = (2, 1, 3, 0)


def kernel(
    hidden_hbm,
    table_hbm,
    ids_hbm,
    targets_hbm,
    input_hbm,
    proj_hbm,
    loss_ref,
    grad_ref,
    low_hbm,
    hidden_ref,
    ids_ref,
    targets_ref,
    input_ref,
    low_ref,
    table,
    proj,
    zraw,
    ipz,
    hall,
    ipy,
    ipx,
    idbuf,
    arbuf,
    capped_s,
    expo_s,
    dmat,
    scale,
    sib_out,
    sib_in,
    acc,
    tsib_out,
    tsib_in,
    tacc,
    tin0,
    tin1,
    out1a,
    in1a,
    out1b,
    in1b,
    out2,
    in2,
    out3,
    in3,
    load_sem,
    zs,
    zr,
    ids_s,
    ids_r,
    ars,
    arr,
    ags,
    agr,
    css,
    csr,
    ips,
    ipr,
    xs,
    xr,
    txs,
    txr,
    ts,
    tr,
    r1s,
    r1r,
    r2s,
    r2r,
    r3s,
    r3r,
):
    sec = lax.axis_index("section")
    voc = lax.axis_index("vocab")
    y = sec // 2
    x = voc // 8
    z = (sec % 2) * 4 + (voc // 2) % 4
    c = voc % 2

    def dev(px, py, pz, pc):
        return {"section": py * 2 + pz // 4, "vocab": (px * 4 + pz % 4) * 2 + pc}

    zc = [
        dev(x, y, (z + dz) % NZ, (c + dc) % 2)
        for dc in range(2)
        for dz in range(NZ)
        if dz or dc
    ]
    xy = [
        dev((x + dx) % NX, (y + dy) % NY, z, c)
        for dx in range(NX)
        for dy in range(NY)
        if dx or dy
    ]
    sibling = dev(x, y, z, (c + 1) % 2)

    def xpeer(d):
        return dev((x + d) % NX, y, z, c)

    def ypeer(d):
        return dev(x, (y + d) % NY, z, c)

    def zpeer(d):
        return dev(x, y, (z + d) % NZ, c)

    started = []

    def send(src, dst, sems, slot, to):
        copy = pltpu.make_async_remote_copy(
            src_ref=src,
            dst_ref=dst,
            send_sem=sems[0].at[slot],
            recv_sem=sems[1].at[slot],
            device_id=to,
            device_id_type=MESH,
        )
        copy.start()
        started.append(copy)
        return copy

    def arrive(copies):
        for copy in copies:
            copy.wait_recv()

    barrier = pltpu.get_barrier_semaphore()
    for peer in zc + xy:
        pl.semaphore_signal(barrier, inc=1, device_id=peer, device_id_type=MESH)
    load_small = [
        pltpu.make_async_copy(hidden_hbm, hidden_ref, load_sem.at[2]),
        pltpu.make_async_copy(input_hbm, input_ref, load_sem.at[3]),
        pltpu.make_async_copy(ids_hbm, ids_ref, load_sem.at[4]),
        pltpu.make_async_copy(targets_hbm, targets_ref, load_sem.at[5]),
    ]
    for copy in load_small:
        copy.start()
    load_proj = pltpu.make_async_copy(proj_hbm, proj, load_sem.at[1])
    load_proj.start()
    load_table = pltpu.make_async_copy(table_hbm, table, load_sem.at[0])
    load_table.start()
    for copy in load_small:
        copy.wait()

    half, zz = (z % 4) // 2, z % 2
    base = half * 64 + x * 16 + zz * 8
    lane = lax.broadcasted_iota(jnp.int32, (1, 256), 1)
    tvec = jnp.zeros((1, 256), jnp.int32)
    ivec = jnp.zeros((1, 256), jnp.int32)
    for i in range(8):
        here = lane == base + i
        tvec = jnp.where(here, targets_ref[i], tvec)
        ivec = jnp.where(here, ids_ref[i], ivec)
    mine = z < 4
    idbuf[0, :, 0:256] = jnp.where(mine, tvec, 0).astype(F32)
    idbuf[0, :, 256:512] = jnp.where(mine, ivec, 0).astype(F32)

    def pack(v):
        return jnp.concatenate([v[:, 0:PIECE], v[:, PIECE:SECT]], axis=0)

    def unpack(v):
        return jnp.concatenate([v[0:8, 0:PIECE], v[8:16, 0:PIECE]], axis=1)

    zraw[z, :, 0:PIECE] = pack(hidden_ref[...].astype(F32)).astype(BF16)

    pl.semaphore_wait(barrier, len(zc) + len(xy))

    id1 = [
        send(idbuf.at[0], idbuf.at[d], (ids_s, ids_r), d - 1, xpeer(d)) for d in range(1, NX)
    ]
    zcopies = [send(zraw.at[z], zraw.at[z], (zs, zr), d - 1, zpeer(d)) for d in range(1, NZ)]

    def swap(v):
        return jnp.concatenate(
            [v[:, 128:256], v[:, 0:128], v[:, 384:512], v[:, 256:384]], axis=1
        )

    def sum_zc(buf):
        return jnp.sum(buf[0:8], axis=0) + swap(jnp.sum(buf[8:16], axis=0))

    arrive(id1)
    idbuf[4] = jnp.sum(idbuf[0:4], axis=0)
    id2 = [
        send(idbuf.at[4], idbuf.at[5 + i], (ids_s, ids_r), 3 + i, p) for i, p in enumerate(zc)
    ]

    load_proj.wait()
    ipz[z] = jnp.dot(
        input_ref[...],
        proj[pl.ds(pl.multiple_of(sec * SECT, 64), SECT), :],
        preferred_element_type=F32,
    )

    arrive(zcopies)
    for h in range(2):
        rows = []
        for k in range(2):
            zl = 2 * h + k
            low_part = unpack(zraw[zl].astype(F32))
            high_part = unpack(zraw[zl + 4].astype(F32))
            rows.append(jnp.concatenate([low_part, high_part], axis=1))
        hall[0, h, y, x] = jnp.concatenate(rows, axis=0).astype(BF16)

    ag = (ags, agr)
    near = {}
    far = {}

    def spread(j):
        bx, by = (x + 4 - j) % NX, (y + 4 - j) % NY
        for d in (1, 3, 2):
            far[0, j, d] = send(hall.at[0, 0, y, bx], hall.at[0, 0, y, bx], ag, 6 + 3 * j + d - 1, ypeer(d))
            far[1, j, d] = send(hall.at[0, 1, by, x], hall.at[0, 1, by, x], ag, 18 + 3 * j + d - 1, xpeer(d))

    for d in (1, 3, 2):
        near[0, d] = send(hall.at[0, 0, y, x], hall.at[0, 0, y, x], ag, d - 1, xpeer(d))
        near[1, d] = send(hall.at[0, 1, y, x], hall.at[0, 1, y, x], ag, 2 + d, ypeer(d))
    spread(0)
    ip = (ips, ipr)
    ipzc = [send(ipz.at[z], ipz.at[z], ip, d - 1, zpeer(d)) for d in range(1, NZ)]
    def sum_ipz():
        arrive(ipzc)
        for h in range(2):
            ipy[y, h] = jnp.concatenate(
                [ipz[2 * h] + ipz[2 * h + 4], ipz[2 * h + 1] + ipz[2 * h + 5]], axis=0
            ).astype(BF16)
        return [send(ipy.at[y], ipy.at[y], ip, 6 + d, ypeer(d)) for d in range(1, 4)]

    load_table.wait()
    arrive(id2)
    idvec = sum_zc(idbuf[4:20])
    targets = idvec[:, 0:256].astype(jnp.int32)
    ids = idvec[:, 256:512].astype(jnp.int32)
    offset = (voc * 8 + sec) * ROWS
    row = offset + lax.broadcasted_iota(jnp.int32, (ROWS, 256), 0)

    dmat[...] = (row == targets).astype(F32).astype(BF16).T
    tcross = []

    def target_rows(k):
        yy = (y + FAR[k]) % NY
        part = jnp.dot(
            dmat[...],
            table[:, pl.ds(pl.multiple_of(yy * QUARTER, 128), QUARTER)],
            preferred_element_type=F32,
        ).astype(BF16)
        tsib_out[k] = part[128:256].reshape(2, NX, 16, QUARTER)
        tcross.append(send(tsib_out.at[k], tsib_in.at[k], (txs, txr), k, sibling))
        tacc[k] = part[0:128].reshape(2, NX, 16, QUARTER)

    target_rows(0)
    for j in (1, 3, 2):
        arrive([near[0, j], near[1, j]])
        spread(j)
    for k in range(1, 4):
        target_rows(k)

    cross = []

    def group(j):
        bx, by = (x + 4 - j) % NX, (y + 4 - j) % NY
        arrive([far[h, j, d] for h in range(2) for d in range(1, 4)])
        cross.append(send(hall.at[0, 0, :, bx], hall.at[1, 0, :, bx], (css, csr), 2 * j, sibling))
        cross.append(send(hall.at[0, 1, by], hall.at[1, 1, by], (css, csr), 2 * j + 1, sibling))

    group(0)
    ipyc = sum_ipz()
    for k in range(4):
        arrive([tcross[k]])
        tacc[k] = tacc[k] + tsib_in[k]
    group(1)
    group(3)
    group(2)

    tfirst = []
    for k in range(3):
        tfirst.append(send(tacc.at[k, 0], tin0.at[k], (ts, tr), k, ypeer(FAR[k])))
        xx = (x + FAR[k]) % NX
        tfirst.append(send(tacc.at[:, 1, xx], tin1.at[k], (ts, tr), 3 + k, xpeer(FAR[k])))
    arrive(cross)

    def tokens_of(yy):
        return jnp.concatenate(
            [hall[p, h, yy].reshape(64, QUARTER) for p in range(2) for h in range(2)], axis=0
        )

    raw = jnp.zeros((ROWS, 256), F32)
    for yy in range(4):
        raw += lax.dot_general(
            table[:, yy * QUARTER : (yy + 1) * QUARTER],
            tokens_of(yy),
            (((1,), (1,)), ((), ())),
            preferred_element_type=F32,
        )
    capped = 30.0 * jnp.tanh(raw / 30.0)
    expo = jnp.exp(capped)
    hit = row == targets
    capped_s[...] = capped
    expo_s[...] = expo
    arbuf[0, :, 0:256] = jnp.sum(expo, axis=0, keepdims=True)
    arbuf[0, :, 256:512] = jnp.sum(jnp.where(hit, capped, 0.0), axis=0, keepdims=True)
    dmat[...] = jnp.where(hit, 0.0, expo * (1.0 - (capped / 30.0) ** 2)).astype(BF16).T
    r1 = (r1s, r1r)
    first0 = {}
    first1 = {}
    crossed = []

    def first_sends(k):
        arrive([crossed[k]])
        acc[k] = acc[k] + sib_in[k].astype(F32)
        for j in range(3):
            dx = FAR[j]
            xx = (x + dx) % NX
            out1b[k, j] = acc[k, 1, xx].astype(BF16)
            first1[k, j] = send(out1b.at[k, j], in1b.at[k, j], r1, 12 + 3 * k + j, xpeer(dx))
            if k < 3:
                out1a[k, j] = acc[k, 0, xx].astype(BF16)
                first0[k, j] = send(out1a.at[k, j], in1a.at[k, j], r1, 4 * k + j, ypeer(FAR[k]))

    def columns(k):
        yy = (y + FAR[k]) % NY
        return table[:, pl.ds(pl.multiple_of(yy * QUARTER, 128), QUARTER)]

    def sib_part(k):
        part = jnp.dot(dmat[128:256], columns(k), preferred_element_type=F32)
        sib_out[k] = part.astype(BF16).reshape(2, NX, 16, QUARTER)
        crossed.append(send(sib_out.at[k], sib_in.at[k], (xs, xr), k, sibling))

    def own_part(k):
        part = jnp.dot(dmat[0:128], columns(k), preferred_element_type=F32)
        acc[k] = part.reshape(2, NX, 16, QUARTER)

    sib_part(0)
    ar1 = [send(arbuf.at[0], arbuf.at[1 + i], (ars, arr), i, p) for i, p in enumerate(zc)]
    own_part(0)
    sib_part(1)
    first_sends(0)
    own_part(1)
    sib_part(2)
    first_sends(1)
    own_part(2)
    sib_part(3)
    first_sends(2)
    arrive(ar1)
    arbuf[16] = sum_zc(arbuf)
    ar2 = [send(arbuf.at[16], arbuf.at[17 + i], (ars, arr), 15 + i, p) for i, p in enumerate(xy)]
    own_part(3)
    first_sends(3)
    for k in range(3):
        out1a[k, 3] = acc[k, 0, x].astype(BF16)
        first0[k, 3] = send(out1a.at[k, 3], in1a.at[k, 3], r1, 4 * k + 3, ypeer(FAR[k]))

    arrive(ipyc)
    ipx[0, x] = (
        ipy[0].astype(F32) + ipy[1].astype(F32) + ipy[2].astype(F32) + ipy[3].astype(F32)
    ).astype(BF16)
    ipxc = [send(ipx.at[0, x], ipx.at[0, x], ip, 9 + d, xpeer(d)) for d in range(1, 4)]
    hproj = jnp.zeros((256, RANK), F32)
    for yy in range(4):
        hproj += jnp.dot(
            tokens_of(yy), proj[yy * QUARTER : (yy + 1) * QUARTER, :], preferred_element_type=F32
        )
    arrive(ar2)
    sums = jnp.sum(arbuf[16:32], axis=0)
    total, picked = sums[:, 0:256], sums[:, 256:512]
    inverse = 1.0 / total
    target_coef = (jnp.exp(picked) / total - 1.0) * (1.0 - (picked / 30.0) ** 2)
    scale[0] = jnp.broadcast_to(inverse[:, 0:128], (128, 128)).T.reshape(2, NX, 16, 128)
    scale[1] = jnp.broadcast_to(target_coef[:, 0:128], (128, 128)).T.reshape(2, NX, 16, 128)

    def scaled(u, t, h, xx):
        return u * scale[0, h, xx][:, 0:1] + t * scale[1, h, xx][:, 0:1]

    arrive(tfirst)
    r2 = (r2s, r2r)
    second = []
    kept = {}

    def step0(j):
        arrive([first0[k, j] for k in range(3)])
        xx = (x + FAR[j]) % NX
        u = acc[3, 0, xx]
        t = tacc[3, 0, xx].astype(F32)
        for k in range(3):
            u = u + in1a[k, j].astype(F32)
            t = t + tin0[k, xx].astype(F32)
        s = scaled(u, t, 0, xx)
        if j < 3:
            out2[0, j] = s.astype(BF16)
            second.append(send(out2.at[0, j], in2.at[0, j], r2, j, xpeer(FAR[j])))
        else:
            kept[0] = s

    def step1(k):
        arrive([first1[k, j] for j in range(3)])
        u = acc[k, 1, x]
        t = tacc[k, 1, x].astype(F32)
        for j in range(3):
            u = u + in1b[k, j].astype(F32)
            t = t + tin1[j, k].astype(F32)
        s = scaled(u, t, 1, x)
        if k < 3:
            out2[1, k] = s.astype(BF16)
            second.append(send(out2.at[1, k], in2.at[1, k], r2, 3 + k, ypeer(FAR[k])))
        else:
            kept[1] = s

    step1(0)
    step1(1)
    step0(0)
    step1(2)
    step0(1)
    step0(2)
    step1(3)
    step0(3)
    arrive(ipxc)
    ipcross = send(ipx.at[0], ipx.at[1], ip, 13, sibling)

    arrive(second)
    for zl in range(4):
        h = zl // 2
        if zl % 2 == 0:
            whole = kept[h]
            for j in range(3):
                whole = whole + in2[h, j].astype(F32)
        block = whole[8 * (zl % 2) : 8 * (zl % 2) + 8]
        out3[zl, :, 0:PIECE] = pack(block[:, 0:SECT]).astype(BF16)
        out3[zl + 4, :, 0:PIECE] = pack(block[:, SECT:QUARTER]).astype(BF16)
    third = [
        send(out3.at[(z + d) % NZ], in3.at[z], (r3s, r3r), d - 1, zpeer(d)) for d in range(1, NZ)
    ]
    in3[z] = out3[z]

    loss = jnp.log(total) - picked
    for i in range(8):
        loss_ref[i] = jnp.sum(jnp.where(lane == base + i, loss, 0.0))

    def split(v):
        upper = v.astype(BF16)
        return upper, (v - upper.astype(F32)).astype(BF16)

    dlogit_t = (
        (expo_s[...] / total - (row == targets).astype(F32)) * (1.0 - (capped_s[...] / 30.0) ** 2)
    ).astype(BF16)
    arrive([ipcross])
    iproj = jnp.concatenate(
        [
            jnp.concatenate([ipx[p, xx, h] for xx in range(NX)], axis=0)
            for p in range(2)
            for h in range(2)
        ],
        axis=0,
    ).astype(F32)
    hp_hi, hp_lo = split(hproj)
    ip_hi, ip_lo = split(iproj * math.sqrt(NY * QUARTER))
    picks = (row == ids).astype(F32).astype(BF16)
    low_ref[...] = (
        jnp.dot(dlogit_t, hp_hi, preferred_element_type=F32)
        + jnp.dot(dlogit_t, hp_lo, preferred_element_type=F32)
        + jnp.dot(picks, ip_hi, preferred_element_type=F32)
        + jnp.dot(picks, ip_lo, preferred_element_type=F32)
    )
    store_low = pltpu.make_async_copy(low_ref, low_hbm, load_sem.at[6])
    store_low.start()

    arrive(third)
    grad = in3[0].astype(F32)
    for k in range(1, NZ):
        grad = grad + in3[k].astype(F32)
    grad_ref[...] = unpack(grad).astype(BF16)
    store_low.wait()
    for copy in started:
        copy.wait_send()


def hand_over(loss_in, grad_in, low_in, loss_out, grad_out, low_out):
    low_out[...] = low_in[...]
    grad_out[...] = grad_in[...]
    for i in range(8):
        loss_out[i] = loss_in[i]


def per_device(hidden, table, token_ids, targets, input_grad, projection):
    dma = pltpu.SemaphoreType.DMA
    vmem = pl.BlockSpec(memory_space=pltpu.VMEM)
    smem = pl.BlockSpec(memory_space=pltpu.SMEM)
    hbm = pl.BlockSpec(memory_space=pl.ANY)
    shapes = (
        jax.ShapeDtypeStruct((8,), F32),
        jax.ShapeDtypeStruct((8, SECT), BF16),
        jax.ShapeDtypeStruct((ROWS, RANK), F32),
    )

    def blocks(n, kind=BF16):
        return pltpu.VMEM((n, 2, NX, 16, QUARTER), kind)

    def pairs(*counts):
        return [dma((n,)) for n in counts for _ in range(2)]

    outs = pl.pallas_call(
        kernel,
        out_shape=shapes,
        in_specs=[hbm] * 6,
        out_specs=(smem, vmem, hbm),
        scratch_shapes=[
            pltpu.VMEM((8, SECT), BF16),
            pltpu.SMEM((8,), jnp.int32),
            pltpu.SMEM((8,), jnp.int32),
            pltpu.VMEM((8, SECT), BF16),
            pltpu.VMEM((ROWS, RANK), F32),
            pltpu.VMEM((ROWS, NY * QUARTER), BF16),
            pltpu.VMEM((NY * QUARTER, RANK), BF16),
            pltpu.VMEM((NZ, 16, 384), BF16),
            pltpu.VMEM((NZ, 8, RANK), F32),
            pltpu.VMEM((2, 2, NY, NX, 16, QUARTER), BF16),
            pltpu.VMEM((NY, 2, 16, RANK), BF16),
            pltpu.VMEM((2, NX, 2, 16, RANK), BF16),
            pltpu.VMEM((20, 1, 512), F32),
            pltpu.VMEM((32, 1, 512), F32),
            pltpu.VMEM((ROWS, 256), F32),
            pltpu.VMEM((ROWS, 256), F32),
            pltpu.VMEM((256, ROWS), BF16),
            pltpu.VMEM((2, 2, NX, 16, 128), F32),
            blocks(4),
            blocks(4),
            blocks(4, F32),
            blocks(4),
            blocks(4),
            blocks(4),
            pltpu.VMEM((3, NX, 16, QUARTER), BF16),
            pltpu.VMEM((3, 4, 16, QUARTER), BF16),
            pltpu.VMEM((3, 4, 16, QUARTER), BF16),
            pltpu.VMEM((3, 4, 16, QUARTER), BF16),
            pltpu.VMEM((4, 3, 16, QUARTER), BF16),
            pltpu.VMEM((4, 3, 16, QUARTER), BF16),
            pltpu.VMEM((2, 3, 16, QUARTER), BF16),
            pltpu.VMEM((2, 3, 16, QUARTER), BF16),
            pltpu.VMEM((NZ, 16, 384), BF16),
            pltpu.VMEM((NZ, 16, 384), BF16),
            dma((7,)),
            *pairs(7, 18, 30, 30, 8, 14, 4, 4, 6, 24, 6, 7),
        ],
        compiler_params=pltpu.CompilerParams(
            collective_id=0, has_side_effects=True, vmem_limit_bytes=58 * 2**20
        ),
        cost_estimate=pl.CostEstimate(
            flops=8 * 10**9, bytes_accessed=13 * 10**6, transcendentals=512000
        ),
    )(hidden, table, token_ids, targets, input_grad, projection)
    return pl.pallas_call(
        hand_over,
        out_shape=shapes,
        in_specs=[smem, vmem, vmem],
        out_specs=(smem, vmem, vmem),
    )(*outs)


def solution(mesh):
    placed = (
        P("vocab", "section"),
        P(("vocab", "section"), None),
        P("vocab"),
        P("vocab"),
        P("vocab", "section"),
        P(),
    )
    return jax.shard_map(
        per_device,
        mesh=mesh,
        in_specs=placed,
        out_specs=(P("vocab"), P("vocab", "section"), P(("vocab", "section"), None)),
        check_vma=False,
    )
```

```python
import math

import jax
import jax.numpy as jnp
from jax import lax
from jax.experimental import pallas as pl
from jax.experimental.pallas import tpu as pltpu
from jax.sharding import PartitionSpec as P

MESH = pl.DeviceIdType.MESH
F32 = jnp.float32
BF16 = jnp.bfloat16
NY = 4
NX = 4
NZ = 8
QUARTER = 1152
SECT = 576
PIECE = 288
ROWS = 1000
RANK = 256
FAR = (2, 1, 3, 0)
ZFAR = (4, 3, 5, 2, 6, 1, 7)


def kernel(
    hidden_hbm,
    table_hbm,
    ids_hbm,
    targets_hbm,
    input_hbm,
    proj_hbm,
    loss_ref,
    grad_ref,
    low_hbm,
    hidden_ref,
    ids_ref,
    targets_ref,
    input_ref,
    low_ref,
    table,
    proj,
    zraw,
    ipz,
    hall,
    ipy,
    ipx,
    idbuf,
    arbuf,
    capped_s,
    expo_s,
    dmat,
    scale,
    sib_out,
    sib_in,
    acc,
    tsib_out,
    tsib_in,
    tacc,
    tin0,
    tin1,
    out1a,
    in1a,
    out1b,
    in1b,
    out2,
    in2,
    out3,
    in3,
    load_sem,
    zs,
    zr,
    ids_s,
    ids_r,
    ars,
    arr,
    ags,
    agr,
    css,
    csr,
    ips,
    ipr,
    xs,
    xr,
    txs,
    txr,
    ts,
    tr,
    r1s,
    r1r,
    r2s,
    r2r,
    r3s,
    r3r,
):
    sec = lax.axis_index("section")
    voc = lax.axis_index("vocab")
    y = sec // 2
    x = voc // 8
    z = (sec % 2) * 4 + (voc // 2) % 4
    c = voc % 2

    def dev(px, py, pz, pc):
        return {"section": py * 2 + pz // 4, "vocab": (px * 4 + pz % 4) * 2 + pc}

    zc = [
        dev(x, y, (z + dz) % NZ, (c + dc) % 2)
        for dc in range(2)
        for dz in range(NZ)
        if dz or dc
    ]
    xy = [
        dev((x + dx) % NX, (y + dy) % NY, z, c)
        for dx in range(NX)
        for dy in range(NY)
        if dx or dy
    ]
    sibling = dev(x, y, z, (c + 1) % 2)

    def xpeer(d):
        return dev((x + d) % NX, y, z, c)

    def ypeer(d):
        return dev(x, (y + d) % NY, z, c)

    def zpeer(d):
        return dev(x, y, (z + d) % NZ, c)

    started = []

    def send(src, dst, sems, slot, to):
        copy = pltpu.make_async_remote_copy(
            src_ref=src,
            dst_ref=dst,
            send_sem=sems[0].at[slot],
            recv_sem=sems[1].at[slot],
            device_id=to,
            device_id_type=MESH,
        )
        copy.start()
        started.append(copy)
        return copy

    def arrive(copies):
        for copy in copies:
            copy.wait_recv()

    barrier = pltpu.get_barrier_semaphore()
    for peer in zc + xy:
        pl.semaphore_signal(barrier, inc=1, device_id=peer, device_id_type=MESH)
    load_small = [
        pltpu.make_async_copy(hidden_hbm, hidden_ref, load_sem.at[2]),
        pltpu.make_async_copy(input_hbm, input_ref, load_sem.at[3]),
        pltpu.make_async_copy(ids_hbm, ids_ref, load_sem.at[4]),
        pltpu.make_async_copy(targets_hbm, targets_ref, load_sem.at[5]),
    ]
    for copy in load_small:
        copy.start()
    load_proj = pltpu.make_async_copy(proj_hbm, proj, load_sem.at[1])
    load_proj.start()
    load_table = pltpu.make_async_copy(table_hbm, table, load_sem.at[0])
    load_table.start()
    for copy in load_small:
        copy.wait()

    half, zz = (z % 4) // 2, z % 2
    base = half * 64 + x * 16 + zz * 8
    lane = lax.broadcasted_iota(jnp.int32, (1, 256), 1)
    tvec = jnp.zeros((1, 256), jnp.int32)
    ivec = jnp.zeros((1, 256), jnp.int32)
    for i in range(8):
        here = lane == base + i
        tvec = jnp.where(here, targets_ref[i], tvec)
        ivec = jnp.where(here, ids_ref[i], ivec)
    mine = z < 4
    idbuf[0, :, 0:256] = jnp.where(mine, tvec, 0).astype(F32)
    idbuf[0, :, 256:512] = jnp.where(mine, ivec, 0).astype(F32)

    def pack(v):
        return jnp.concatenate([v[:, 0:PIECE], v[:, PIECE:SECT]], axis=0)

    def unpack(v):
        return jnp.concatenate([v[0:8, 0:PIECE], v[8:16, 0:PIECE]], axis=1)

    zraw[z, :, 0:PIECE] = pack(hidden_ref[...].astype(F32)).astype(BF16)

    pl.semaphore_wait(barrier, len(zc) + len(xy))

    id1 = [
        send(idbuf.at[0], idbuf.at[d], (ids_s, ids_r), d - 1, xpeer(d)) for d in range(1, NX)
    ]
    zcopies = [send(zraw.at[z], zraw.at[z], (zs, zr), d - 1, zpeer(d)) for d in ZFAR]

    def swap(v):
        return jnp.concatenate(
            [v[:, 128:256], v[:, 0:128], v[:, 384:512], v[:, 256:384]], axis=1
        )

    def sum_zc(buf):
        return jnp.sum(buf[0:8], axis=0) + swap(jnp.sum(buf[8:16], axis=0))

    arrive(id1)
    idbuf[4] = jnp.sum(idbuf[0:4], axis=0)
    id2 = [
        send(idbuf.at[4], idbuf.at[5 + i], (ids_s, ids_r), 3 + i, p) for i, p in enumerate(zc)
    ]

    load_proj.wait()
    ipz[z] = jnp.dot(
        input_ref[...],
        proj[pl.ds(pl.multiple_of(sec * SECT, 64), SECT), :],
        preferred_element_type=F32,
    )

    arrive(zcopies)
    for h in range(2):
        rows = []
        for k in range(2):
            zl = 2 * h + k
            low_part = unpack(zraw[zl].astype(F32))
            high_part = unpack(zraw[zl + 4].astype(F32))
            rows.append(jnp.concatenate([low_part, high_part], axis=1))
        hall[0, h, y, x] = jnp.concatenate(rows, axis=0).astype(BF16)

    ag = (ags, agr)
    near = {}
    far = {}

    def spread(j):
        bx, by = (x + 4 - j) % NX, (y + 4 - j) % NY
        for d in (1, 3, 2):
            far[0, j, d] = send(hall.at[0, 0, y, bx], hall.at[0, 0, y, bx], ag, 6 + 3 * j + d - 1, ypeer(d))
            far[1, j, d] = send(hall.at[0, 1, by, x], hall.at[0, 1, by, x], ag, 18 + 3 * j + d - 1, xpeer(d))

    for d in (1, 3, 2):
        near[0, d] = send(hall.at[0, 0, y, x], hall.at[0, 0, y, x], ag, d - 1, xpeer(d))
        near[1, d] = send(hall.at[0, 1, y, x], hall.at[0, 1, y, x], ag, 2 + d, ypeer(d))
    spread(0)
    ip = (ips, ipr)
    ipzc = [send(ipz.at[z], ipz.at[z], ip, d - 1, zpeer(d)) for d in range(1, NZ)]
    def sum_ipz():
        arrive(ipzc)
        for h in range(2):
            ipy[y, h] = jnp.concatenate(
                [ipz[2 * h] + ipz[2 * h + 4], ipz[2 * h + 1] + ipz[2 * h + 5]], axis=0
            ).astype(BF16)
        return [send(ipy.at[y], ipy.at[y], ip, 6 + d, ypeer(d)) for d in range(1, 4)]

    for j in (1, 3, 2):
        arrive([near[0, j], near[1, j]])
        spread(j)
    load_table.wait()
    arrive(id2)
    idvec = sum_zc(idbuf[4:20])
    targets = idvec[:, 0:256].astype(jnp.int32)
    ids = idvec[:, 256:512].astype(jnp.int32)
    offset = (voc * 8 + sec) * ROWS
    row = offset + lax.broadcasted_iota(jnp.int32, (ROWS, 256), 0)

    dmat[...] = (row == targets).astype(F32).astype(BF16).T
    tcross = []

    def target_rows(k):
        yy = (y + FAR[k]) % NY
        part = jnp.dot(
            dmat[...],
            table[:, pl.ds(pl.multiple_of(yy * QUARTER, 128), QUARTER)],
            preferred_element_type=F32,
        ).astype(BF16)
        tsib_out[k] = part[128:256].reshape(2, NX, 16, QUARTER)
        tcross.append(send(tsib_out.at[k], tsib_in.at[k], (txs, txr), k, sibling))
        tacc[k] = part[0:128].reshape(2, NX, 16, QUARTER)

    for k in range(3):
        target_rows(k)

    cross = []

    def group(j):
        bx, by = (x + 4 - j) % NX, (y + 4 - j) % NY
        arrive([far[h, j, d] for h in range(2) for d in range(1, 4)])
        cross.append(send(hall.at[0, 0, :, bx], hall.at[1, 0, :, bx], (css, csr), 2 * j, sibling))
        cross.append(send(hall.at[0, 1, by], hall.at[1, 1, by], (css, csr), 2 * j + 1, sibling))

    group(0)
    group(1)
    target_rows(3)
    group(3)
    group(2)

    for k in range(4):
        arrive([tcross[k]])
        tacc[k] = tacc[k] + tsib_in[k]
    tfirst = []
    for k in range(3):
        tfirst.append(send(tacc.at[k, 0], tin0.at[k], (ts, tr), k, ypeer(FAR[k])))
        xx = (x + FAR[k]) % NX
        tfirst.append(send(tacc.at[:, 1, xx], tin1.at[k], (ts, tr), 3 + k, xpeer(FAR[k])))
    ipyc = sum_ipz()
    arrive(cross)

    def tokens_of(yy):
        return jnp.concatenate(
            [hall[p, h, yy].reshape(64, QUARTER) for p in range(2) for h in range(2)], axis=0
        )

    raw = jnp.zeros((ROWS, 256), F32)
    for yy in range(4):
        raw += lax.dot_general(
            table[:, yy * QUARTER : (yy + 1) * QUARTER],
            tokens_of(yy),
            (((1,), (1,)), ((), ())),
            preferred_element_type=F32,
        )
    capped = 30.0 * jnp.tanh(raw / 30.0)
    expo = jnp.exp(capped)
    hit = row == targets
    capped_s[...] = capped
    expo_s[...] = expo
    arbuf[0, :, 0:256] = jnp.sum(expo, axis=0, keepdims=True)
    arbuf[0, :, 256:512] = jnp.sum(jnp.where(hit, capped, 0.0), axis=0, keepdims=True)
    dmat[...] = jnp.where(hit, 0.0, expo * (1.0 - (capped / 30.0) ** 2)).astype(BF16).T
    r1 = (r1s, r1r)
    first0 = {}
    first1 = {}
    crossed = []

    def first_sends(k):
        arrive([crossed[k]])
        acc[k] = acc[k] + sib_in[k].astype(F32)
        for j in range(3):
            dx = FAR[j]
            xx = (x + dx) % NX
            out1b[k, j] = acc[k, 1, xx].astype(BF16)
            first1[k, j] = send(out1b.at[k, j], in1b.at[k, j], r1, 12 + 3 * k + j, xpeer(dx))
            if k < 3:
                out1a[k, j] = acc[k, 0, xx].astype(BF16)
                first0[k, j] = send(out1a.at[k, j], in1a.at[k, j], r1, 4 * k + j, ypeer(FAR[k]))

    def columns(k):
        yy = (y + FAR[k]) % NY
        return table[:, pl.ds(pl.multiple_of(yy * QUARTER, 128), QUARTER)]

    def sib_part(k):
        part = jnp.dot(dmat[128:256], columns(k), preferred_element_type=F32)
        sib_out[k] = part.astype(BF16).reshape(2, NX, 16, QUARTER)
        crossed.append(send(sib_out.at[k], sib_in.at[k], (xs, xr), k, sibling))

    def own_part(k):
        part = jnp.dot(dmat[0:128], columns(k), preferred_element_type=F32)
        acc[k] = part.reshape(2, NX, 16, QUARTER)

    sib_part(0)
    ar1 = [send(arbuf.at[0], arbuf.at[1 + i], (ars, arr), i, p) for i, p in enumerate(zc)]
    own_part(0)
    sib_part(1)
    first_sends(0)
    own_part(1)
    sib_part(2)
    first_sends(1)
    own_part(2)
    sib_part(3)
    first_sends(2)
    arrive(ar1)
    arbuf[16] = sum_zc(arbuf)
    ar2 = [send(arbuf.at[16], arbuf.at[17 + i], (ars, arr), 15 + i, p) for i, p in enumerate(xy)]
    own_part(3)
    first_sends(3)
    for k in range(3):
        out1a[k, 3] = acc[k, 0, x].astype(BF16)
        first0[k, 3] = send(out1a.at[k, 3], in1a.at[k, 3], r1, 4 * k + 3, ypeer(FAR[k]))

    arrive(ipyc)
    ipx[0, x] = (
        ipy[0].astype(F32) + ipy[1].astype(F32) + ipy[2].astype(F32) + ipy[3].astype(F32)
    ).astype(BF16)
    ipxc = [send(ipx.at[0, x], ipx.at[0, x], ip, 9 + d, xpeer(d)) for d in range(1, 4)]
    hproj = jnp.zeros((256, RANK), F32)
    for yy in range(4):
        hproj += jnp.dot(
            tokens_of(yy), proj[yy * QUARTER : (yy + 1) * QUARTER, :], preferred_element_type=F32
        )
    arrive(ar2)
    sums = jnp.sum(arbuf[16:32], axis=0)
    total, picked = sums[:, 0:256], sums[:, 256:512]
    inverse = 1.0 / total
    target_coef = (jnp.exp(picked) / total - 1.0) * (1.0 - (picked / 30.0) ** 2)
    scale[0] = jnp.broadcast_to(inverse[:, 0:128], (128, 128)).T.reshape(2, NX, 16, 128)
    scale[1] = jnp.broadcast_to(target_coef[:, 0:128], (128, 128)).T.reshape(2, NX, 16, 128)

    def scaled(u, t, h, xx):
        return u * scale[0, h, xx][:, 0:1] + t * scale[1, h, xx][:, 0:1]

    arrive(tfirst)
    r2 = (r2s, r2r)
    second = []
    kept = {}

    def step0(j):
        arrive([first0[k, j] for k in range(3)])
        xx = (x + FAR[j]) % NX
        u = acc[3, 0, xx]
        t = tacc[3, 0, xx].astype(F32)
        for k in range(3):
            u = u + in1a[k, j].astype(F32)
            t = t + tin0[k, xx].astype(F32)
        s = scaled(u, t, 0, xx)
        if j < 3:
            out2[0, j] = s.astype(BF16)
            second.append(send(out2.at[0, j], in2.at[0, j], r2, j, xpeer(FAR[j])))
        else:
            kept[0] = s

    def step1(k):
        arrive([first1[k, j] for j in range(3)])
        u = acc[k, 1, x]
        t = tacc[k, 1, x].astype(F32)
        for j in range(3):
            u = u + in1b[k, j].astype(F32)
            t = t + tin1[j, k].astype(F32)
        s = scaled(u, t, 1, x)
        if k < 3:
            out2[1, k] = s.astype(BF16)
            second.append(send(out2.at[1, k], in2.at[1, k], r2, 3 + k, ypeer(FAR[k])))
        else:
            kept[1] = s

    step1(0)
    step1(1)
    step0(0)
    step1(2)
    step0(1)
    step0(2)
    step1(3)
    step0(3)
    arrive(ipxc)
    ipcross = send(ipx.at[0], ipx.at[1], ip, 13, sibling)

    arrive(second)
    for zl in range(4):
        h = zl // 2
        if zl % 2 == 0:
            whole = kept[h]
            for j in range(3):
                whole = whole + in2[h, j].astype(F32)
        block = whole[8 * (zl % 2) : 8 * (zl % 2) + 8]
        out3[zl, :, 0:PIECE] = pack(block[:, 0:SECT]).astype(BF16)
        out3[zl + 4, :, 0:PIECE] = pack(block[:, SECT:QUARTER]).astype(BF16)
    third = [
        send(out3.at[(z + d) % NZ], in3.at[z], (r3s, r3r), d - 1, zpeer(d)) for d in ZFAR
    ]
    in3[z] = out3[z]

    loss = jnp.log(total) - picked
    for i in range(8):
        loss_ref[i] = jnp.sum(jnp.where(lane == base + i, loss, 0.0))

    def split(v):
        upper = v.astype(BF16)
        return upper, (v - upper.astype(F32)).astype(BF16)

    dlogit_t = (
        (expo_s[...] / total - (row == targets).astype(F32)) * (1.0 - (capped_s[...] / 30.0) ** 2)
    ).astype(BF16)
    arrive([ipcross])
    iproj = jnp.concatenate(
        [
            jnp.concatenate([ipx[p, xx, h] for xx in range(NX)], axis=0)
            for p in range(2)
            for h in range(2)
        ],
        axis=0,
    ).astype(F32)
    hp_hi, hp_lo = split(hproj)
    ip_hi, ip_lo = split(iproj * math.sqrt(NY * QUARTER))
    picks = (row == ids).astype(F32).astype(BF16)
    low_ref[...] = (
        jnp.dot(dlogit_t, hp_hi, preferred_element_type=F32)
        + jnp.dot(dlogit_t, hp_lo, preferred_element_type=F32)
        + jnp.dot(picks, ip_hi, preferred_element_type=F32)
        + jnp.dot(picks, ip_lo, preferred_element_type=F32)
    )
    store_low = pltpu.make_async_copy(low_ref, low_hbm, load_sem.at[6])
    store_low.start()

    arrive(third)
    grad = in3[0].astype(F32)
    for k in range(1, NZ):
        grad = grad + in3[k].astype(F32)
    grad_ref[...] = unpack(grad).astype(BF16)
    store_low.wait()
    for copy in started:
        copy.wait_send()


def hand_over(loss_in, grad_in, low_in, loss_out, grad_out, low_out):
    low_out[...] = low_in[...]
    grad_out[...] = grad_in[...]
    for i in range(8):
        loss_out[i] = loss_in[i]


def per_device(hidden, table, token_ids, targets, input_grad, projection):
    dma = pltpu.SemaphoreType.DMA
    vmem = pl.BlockSpec(memory_space=pltpu.VMEM)
    smem = pl.BlockSpec(memory_space=pltpu.SMEM)
    hbm = pl.BlockSpec(memory_space=pl.ANY)
    shapes = (
        jax.ShapeDtypeStruct((8,), F32),
        jax.ShapeDtypeStruct((8, SECT), BF16),
        jax.ShapeDtypeStruct((ROWS, RANK), F32),
    )

    def blocks(n, kind=BF16):
        return pltpu.VMEM((n, 2, NX, 16, QUARTER), kind)

    def pairs(*counts):
        return [dma((n,)) for n in counts for _ in range(2)]

    outs = pl.pallas_call(
        kernel,
        out_shape=shapes,
        in_specs=[hbm] * 6,
        out_specs=(smem, vmem, hbm),
        scratch_shapes=[
            pltpu.VMEM((8, SECT), BF16),
            pltpu.SMEM((8,), jnp.int32),
            pltpu.SMEM((8,), jnp.int32),
            pltpu.VMEM((8, SECT), BF16),
            pltpu.VMEM((ROWS, RANK), F32),
            pltpu.VMEM((ROWS, NY * QUARTER), BF16),
            pltpu.VMEM((NY * QUARTER, RANK), BF16),
            pltpu.VMEM((NZ, 16, 384), BF16),
            pltpu.VMEM((NZ, 8, RANK), F32),
            pltpu.VMEM((2, 2, NY, NX, 16, QUARTER), BF16),
            pltpu.VMEM((NY, 2, 16, RANK), BF16),
            pltpu.VMEM((2, NX, 2, 16, RANK), BF16),
            pltpu.VMEM((20, 1, 512), F32),
            pltpu.VMEM((32, 1, 512), F32),
            pltpu.VMEM((ROWS, 256), F32),
            pltpu.VMEM((ROWS, 256), F32),
            pltpu.VMEM((256, ROWS), BF16),
            pltpu.VMEM((2, 2, NX, 16, 128), F32),
            blocks(4),
            blocks(4),
            blocks(4, F32),
            blocks(4),
            blocks(4),
            blocks(4),
            pltpu.VMEM((3, NX, 16, QUARTER), BF16),
            pltpu.VMEM((3, 4, 16, QUARTER), BF16),
            pltpu.VMEM((3, 4, 16, QUARTER), BF16),
            pltpu.VMEM((3, 4, 16, QUARTER), BF16),
            pltpu.VMEM((4, 3, 16, QUARTER), BF16),
            pltpu.VMEM((4, 3, 16, QUARTER), BF16),
            pltpu.VMEM((2, 3, 16, QUARTER), BF16),
            pltpu.VMEM((2, 3, 16, QUARTER), BF16),
            pltpu.VMEM((NZ, 16, 384), BF16),
            pltpu.VMEM((NZ, 16, 384), BF16),
            dma((7,)),
            *pairs(7, 18, 30, 30, 8, 14, 4, 4, 6, 24, 6, 7),
        ],
        compiler_params=pltpu.CompilerParams(
            collective_id=0, has_side_effects=True, vmem_limit_bytes=58 * 2**20
        ),
        cost_estimate=pl.CostEstimate(
            flops=8 * 10**9, bytes_accessed=13 * 10**6, transcendentals=512000
        ),
    )(hidden, table, token_ids, targets, input_grad, projection)
    return pl.pallas_call(
        hand_over,
        out_shape=shapes,
        in_specs=[smem, vmem, vmem],
        out_specs=(smem, vmem, vmem),
    )(*outs)


def solution(mesh):
    placed = (
        P("vocab", "section"),
        P(("vocab", "section"), None),
        P("vocab"),
        P("vocab"),
        P("vocab", "section"),
        P(),
    )
    return jax.shard_map(
        per_device,
        mesh=mesh,
        in_specs=placed,
        out_specs=(P("vocab"), P("vocab", "section"), P(("vocab", "section"), None)),
        check_vma=False,
    )
```

```python
import math

import jax
import jax.numpy as jnp
from jax import lax
from jax.experimental import pallas as pl
from jax.experimental.pallas import tpu as pltpu
from jax.sharding import PartitionSpec as P

MESH = pl.DeviceIdType.MESH
F32 = jnp.float32
BF16 = jnp.bfloat16
NY = 4
NX = 4
NZ = 8
QUARTER = 1152
SECT = 576
PIECE = 288
ROWS = 1000
RANK = 256
FAR = (2, 1, 3, 0)
ZFAR = (4, 3, 5, 2, 6, 1, 7)


def kernel(
    hidden_hbm,
    table_hbm,
    ids_hbm,
    targets_hbm,
    input_hbm,
    proj_hbm,
    loss_ref,
    grad_ref,
    low_hbm,
    hidden_ref,
    ids_ref,
    targets_ref,
    input_ref,
    low_ref,
    table,
    proj,
    zraw,
    ipz,
    hall,
    ipy,
    ipx,
    idbuf,
    arbuf,
    capped_s,
    expo_s,
    dmat,
    scale,
    sib_out,
    sib_in,
    acc,
    tsib_out,
    tsib_in,
    tacc,
    tin0,
    tin1,
    out1a,
    in1a,
    out1b,
    in1b,
    out2,
    in2,
    out3,
    in3,
    load_sem,
    zs,
    zr,
    ids_s,
    ids_r,
    ars,
    arr,
    ags,
    agr,
    css,
    csr,
    ips,
    ipr,
    xs,
    xr,
    txs,
    txr,
    ts,
    tr,
    r1s,
    r1r,
    r2s,
    r2r,
    r3s,
    r3r,
):
    sec = lax.axis_index("section")
    voc = lax.axis_index("vocab")
    y = sec // 2
    x = voc // 8
    z = (sec % 2) * 4 + (voc // 2) % 4
    c = voc % 2

    def dev(px, py, pz, pc):
        return {"section": py * 2 + pz // 4, "vocab": (px * 4 + pz % 4) * 2 + pc}

    zc = [
        dev(x, y, (z + dz) % NZ, (c + dc) % 2)
        for dc in range(2)
        for dz in range(NZ)
        if dz or dc
    ]
    xy = [
        dev((x + dx) % NX, (y + dy) % NY, z, c)
        for dx in range(NX)
        for dy in range(NY)
        if dx or dy
    ]
    sibling = dev(x, y, z, (c + 1) % 2)

    def xpeer(d):
        return dev((x + d) % NX, y, z, c)

    def ypeer(d):
        return dev(x, (y + d) % NY, z, c)

    def zpeer(d):
        return dev(x, y, (z + d) % NZ, c)

    started = []

    def send(src, dst, sems, slot, to):
        copy = pltpu.make_async_remote_copy(
            src_ref=src,
            dst_ref=dst,
            send_sem=sems[0].at[slot],
            recv_sem=sems[1].at[slot],
            device_id=to,
            device_id_type=MESH,
        )
        copy.start()
        started.append(copy)
        return copy

    def arrive(copies):
        for copy in copies:
            copy.wait_recv()

    barrier = pltpu.get_barrier_semaphore()
    for peer in zc + xy:
        pl.semaphore_signal(barrier, inc=1, device_id=peer, device_id_type=MESH)
    load_small = [
        pltpu.make_async_copy(hidden_hbm, hidden_ref, load_sem.at[2]),
        pltpu.make_async_copy(input_hbm, input_ref, load_sem.at[3]),
        pltpu.make_async_copy(ids_hbm, ids_ref, load_sem.at[4]),
        pltpu.make_async_copy(targets_hbm, targets_ref, load_sem.at[5]),
    ]
    for copy in load_small:
        copy.start()
    load_proj = pltpu.make_async_copy(proj_hbm, proj, load_sem.at[1])
    load_proj.start()
    load_table = pltpu.make_async_copy(table_hbm, table, load_sem.at[0])
    load_table.start()
    for copy in load_small:
        copy.wait()

    half, zz = (z % 4) // 2, z % 2
    base = half * 64 + x * 16 + zz * 8
    lane = lax.broadcasted_iota(jnp.int32, (1, 256), 1)
    tvec = jnp.zeros((1, 256), jnp.int32)
    ivec = jnp.zeros((1, 256), jnp.int32)
    for i in range(8):
        here = lane == base + i
        tvec = jnp.where(here, targets_ref[i], tvec)
        ivec = jnp.where(here, ids_ref[i], ivec)
    mine = z < 4
    idbuf[0, :, 0:256] = jnp.where(mine, tvec, 0).astype(F32)
    idbuf[0, :, 256:512] = jnp.where(mine, ivec, 0).astype(F32)

    def pack(v):
        return jnp.concatenate([v[:, 0:PIECE], v[:, PIECE:SECT]], axis=0)

    def unpack(v):
        return jnp.concatenate([v[0:8, 0:PIECE], v[8:16, 0:PIECE]], axis=1)

    zraw[z, :, 0:PIECE] = pack(hidden_ref[...].astype(F32)).astype(BF16)

    pl.semaphore_wait(barrier, len(zc) + len(xy))

    id1 = [
        send(idbuf.at[0], idbuf.at[d], (ids_s, ids_r), d - 1, xpeer(d)) for d in range(1, NX)
    ]
    zcopies = [send(zraw.at[z], zraw.at[z], (zs, zr), d - 1, zpeer(d)) for d in ZFAR]

    def swap(v):
        return jnp.concatenate(
            [v[:, 128:256], v[:, 0:128], v[:, 384:512], v[:, 256:384]], axis=1
        )

    def sum_zc(buf):
        return jnp.sum(buf[0:8], axis=0) + swap(jnp.sum(buf[8:16], axis=0))

    arrive(id1)
    idbuf[4] = jnp.sum(idbuf[0:4], axis=0)
    id2 = [
        send(idbuf.at[4], idbuf.at[5 + i], (ids_s, ids_r), 3 + i, p) for i, p in enumerate(zc)
    ]

    load_proj.wait()
    ipz[z] = jnp.dot(
        input_ref[...],
        proj[pl.ds(pl.multiple_of(sec * SECT, 64), SECT), :],
        preferred_element_type=F32,
    )

    arrive(zcopies)
    for h in range(2):
        rows = []
        for k in range(2):
            zl = 2 * h + k
            low_part = unpack(zraw[zl].astype(F32))
            high_part = unpack(zraw[zl + 4].astype(F32))
            rows.append(jnp.concatenate([low_part, high_part], axis=1))
        hall[0, h, y, x] = jnp.concatenate(rows, axis=0).astype(BF16)

    ag = (ags, agr)
    near = {}
    far = {}

    def spread(j):
        bx, by = (x + 4 - j) % NX, (y + 4 - j) % NY
        for d in (1, 3, 2):
            far[0, j, d] = send(hall.at[0, 0, y, bx], hall.at[0, 0, y, bx], ag, 6 + 3 * j + d - 1, ypeer(d))
            far[1, j, d] = send(hall.at[0, 1, by, x], hall.at[0, 1, by, x], ag, 18 + 3 * j + d - 1, xpeer(d))

    for d in (1, 3, 2):
        near[0, d] = send(hall.at[0, 0, y, x], hall.at[0, 0, y, x], ag, d - 1, xpeer(d))
        near[1, d] = send(hall.at[0, 1, y, x], hall.at[0, 1, y, x], ag, 2 + d, ypeer(d))
    spread(0)
    ip = (ips, ipr)
    ipzc = [send(ipz.at[z], ipz.at[z], ip, d - 1, zpeer(d)) for d in range(1, NZ)]
    def sum_ipz():
        arrive(ipzc)
        for h in range(2):
            ipy[y, h] = jnp.concatenate(
                [ipz[2 * h] + ipz[2 * h + 4], ipz[2 * h + 1] + ipz[2 * h + 5]], axis=0
            ).astype(BF16)
        return [send(ipy.at[y], ipy.at[y], ip, 6 + d, ypeer(d)) for d in range(1, 4)]

    for j in (1, 3, 2):
        arrive([near[0, j], near[1, j]])
        spread(j)
    load_table.wait()
    arrive(id2)
    idvec = sum_zc(idbuf[4:20])
    targets = idvec[:, 0:256].astype(jnp.int32)
    ids = idvec[:, 256:512].astype(jnp.int32)
    offset = (voc * 8 + sec) * ROWS
    row = offset + lax.broadcasted_iota(jnp.int32, (ROWS, 256), 0)

    dmat[...] = (row == targets).astype(F32).astype(BF16).T
    tcross = []

    def target_rows(k):
        yy = (y + FAR[k]) % NY
        part = jnp.dot(
            dmat[...],
            table[:, pl.ds(pl.multiple_of(yy * QUARTER, 128), QUARTER)],
            preferred_element_type=F32,
        ).astype(BF16)
        tsib_out[k] = part[128:256].reshape(2, NX, 16, QUARTER)
        tcross.append(send(tsib_out.at[k], tsib_in.at[k], (txs, txr), k, sibling))
        tacc[k] = part[0:128].reshape(2, NX, 16, QUARTER)

    for k in range(3):
        target_rows(k)

    cross = []

    def group(j):
        bx, by = (x + 4 - j) % NX, (y + 4 - j) % NY
        arrive([far[h, j, d] for h in range(2) for d in range(1, 4)])
        cross.append(send(hall.at[0, 0, :, bx], hall.at[1, 0, :, bx], (css, csr), 2 * j, sibling))
        cross.append(send(hall.at[0, 1, by], hall.at[1, 1, by], (css, csr), 2 * j + 1, sibling))

    group(0)
    group(1)
    target_rows(3)
    group(3)
    group(2)

    for k in range(4):
        arrive([tcross[k]])
        tacc[k] = tacc[k] + tsib_in[k]
    tfirst = []
    for k in range(3):
        tfirst.append(send(tacc.at[k, 0], tin0.at[k], (ts, tr), k, ypeer(FAR[k])))
        xx = (x + FAR[k]) % NX
        tfirst.append(send(tacc.at[:, 1, xx], tin1.at[k], (ts, tr), 3 + k, xpeer(FAR[k])))
    ipyc = sum_ipz()
    arrive(cross)

    def tokens_of(yy):
        return jnp.concatenate(
            [hall[p, h, yy].reshape(64, QUARTER) for p in range(2) for h in range(2)], axis=0
        )

    raw = jnp.zeros((ROWS, 256), F32)
    for yy in range(4):
        raw += lax.dot_general(
            table[:, yy * QUARTER : (yy + 1) * QUARTER],
            tokens_of(yy),
            (((1,), (1,)), ((), ())),
            preferred_element_type=F32,
        )
    capped = 30.0 * jnp.tanh(raw / 30.0)
    expo = jnp.exp(capped)
    hit = row == targets
    capped_s[...] = capped
    expo_s[...] = expo
    arbuf[0, :, 0:256] = jnp.sum(expo, axis=0, keepdims=True)
    arbuf[0, :, 256:512] = jnp.sum(jnp.where(hit, capped, 0.0), axis=0, keepdims=True)
    dmat[...] = jnp.where(hit, 0.0, expo * (1.0 - (capped / 30.0) ** 2)).astype(BF16).T
    r1 = (r1s, r1r)
    first0 = {}
    first1 = {}
    crossed = []

    def first_sends(k):
        arrive([crossed[k]])
        acc[k] = acc[k] + sib_in[k].astype(F32)
        for j in range(3):
            dx = FAR[j]
            xx = (x + dx) % NX
            out1b[k, j] = acc[k, 1, xx].astype(BF16)
            first1[k, j] = send(out1b.at[k, j], in1b.at[k, j], r1, 12 + 3 * k + j, xpeer(dx))
            if k < 3:
                out1a[k, j] = acc[k, 0, xx].astype(BF16)
                first0[k, j] = send(out1a.at[k, j], in1a.at[k, j], r1, 4 * k + j, ypeer(FAR[k]))

    def columns(k):
        yy = (y + FAR[k]) % NY
        return table[:, pl.ds(pl.multiple_of(yy * QUARTER, 128), QUARTER)]

    def sib_part(k):
        part = jnp.dot(dmat[128:256], columns(k), preferred_element_type=F32)
        sib_out[k] = part.astype(BF16).reshape(2, NX, 16, QUARTER)
        crossed.append(send(sib_out.at[k], sib_in.at[k], (xs, xr), k, sibling))

    def own_part(k):
        part = jnp.dot(dmat[0:128], columns(k), preferred_element_type=F32)
        acc[k] = part.reshape(2, NX, 16, QUARTER)

    sib_part(0)
    ar1 = [send(arbuf.at[0], arbuf.at[1 + i], (ars, arr), i, p) for i, p in enumerate(zc)]
    own_part(0)
    sib_part(1)
    first_sends(0)
    own_part(1)
    sib_part(2)
    first_sends(1)
    own_part(2)
    sib_part(3)
    first_sends(2)
    arrive(ar1)
    arbuf[16] = sum_zc(arbuf)
    ar2 = [send(arbuf.at[16], arbuf.at[17 + i], (ars, arr), 15 + i, p) for i, p in enumerate(xy)]
    own_part(3)
    first_sends(3)
    for k in range(3):
        out1a[k, 3] = acc[k, 0, x].astype(BF16)
        first0[k, 3] = send(out1a.at[k, 3], in1a.at[k, 3], r1, 4 * k + 3, ypeer(FAR[k]))

    arrive(ipyc)
    ipx[0, x] = (
        ipy[0].astype(F32) + ipy[1].astype(F32) + ipy[2].astype(F32) + ipy[3].astype(F32)
    ).astype(BF16)
    ipxc = [send(ipx.at[0, x], ipx.at[0, x], ip, 9 + d, xpeer(d)) for d in range(1, 4)]
    hproj = jnp.zeros((256, RANK), F32)
    for yy in range(4):
        hproj += jnp.dot(
            tokens_of(yy), proj[yy * QUARTER : (yy + 1) * QUARTER, :], preferred_element_type=F32
        )
    arrive(ar2)
    sums = jnp.sum(arbuf[16:32], axis=0)
    total, picked = sums[:, 0:256], sums[:, 256:512]
    inverse = 1.0 / total
    target_coef = (jnp.exp(picked) / total - 1.0) * (1.0 - (picked / 30.0) ** 2)
    scale[0] = jnp.broadcast_to(inverse[:, 0:128], (128, 128)).T.reshape(2, NX, 16, 128)
    scale[1] = jnp.broadcast_to(target_coef[:, 0:128], (128, 128)).T.reshape(2, NX, 16, 128)

    def scaled(u, t, h, xx):
        return u * scale[0, h, xx][:, 0:1] + t * scale[1, h, xx][:, 0:1]

    arrive(tfirst)
    r2 = (r2s, r2r)
    second = []
    kept = {}

    def step0(j):
        arrive([first0[k, j] for k in range(3)])
        xx = (x + FAR[j]) % NX
        u = acc[3, 0, xx]
        t = tacc[3, 0, xx].astype(F32)
        for k in range(3):
            u = u + in1a[k, j].astype(F32)
            t = t + tin0[k, xx].astype(F32)
        s = scaled(u, t, 0, xx)
        if j < 3:
            out2[0, j] = s.astype(BF16)
            second.append(send(out2.at[0, j], in2.at[0, j], r2, j, xpeer(FAR[j])))
        else:
            kept[0] = s

    def step1(k):
        arrive([first1[k, j] for j in range(3)])
        u = acc[k, 1, x]
        t = tacc[k, 1, x].astype(F32)
        for j in range(3):
            u = u + in1b[k, j].astype(F32)
            t = t + tin1[j, k].astype(F32)
        s = scaled(u, t, 1, x)
        if k < 3:
            out2[1, k] = s.astype(BF16)
            second.append(send(out2.at[1, k], in2.at[1, k], r2, 3 + k, ypeer(FAR[k])))
        else:
            kept[1] = s

    step1(0)
    step1(1)
    step0(0)
    step1(2)
    step0(1)
    step0(2)
    step1(3)
    step0(3)
    arrive(ipxc)
    ipcross = send(ipx.at[0], ipx.at[1], ip, 13, sibling)

    arrive(second)
    for zl in range(4):
        h = zl // 2
        if zl % 2 == 0:
            whole = kept[h]
            for j in range(3):
                whole = whole + in2[h, j].astype(F32)
        block = whole[8 * (zl % 2) : 8 * (zl % 2) + 8]
        out3[zl, :, 0:PIECE] = pack(block[:, 0:SECT]).astype(BF16)
        out3[zl + 4, :, 0:PIECE] = pack(block[:, SECT:QUARTER]).astype(BF16)
    third = [
        send(out3.at[(z + d) % NZ], in3.at[z], (r3s, r3r), d - 1, zpeer(d)) for d in ZFAR
    ]
    in3[z] = out3[z]

    loss = jnp.log(total) - picked
    for i in range(8):
        loss_ref[i] = jnp.sum(jnp.where(lane == base + i, loss, 0.0))

    def split(v):
        upper = v.astype(BF16)
        return upper, (v - upper.astype(F32)).astype(BF16)

    dlogit_t = (
        (expo_s[...] / total - (row == targets).astype(F32)) * (1.0 - (capped_s[...] / 30.0) ** 2)
    ).astype(BF16)
    arrive([ipcross])
    iproj = jnp.concatenate(
        [
            jnp.concatenate([ipx[p, xx, h] for xx in range(NX)], axis=0)
            for p in range(2)
            for h in range(2)
        ],
        axis=0,
    ).astype(F32)
    hp_hi, hp_lo = split(hproj)
    ip_hi, ip_lo = split(iproj * math.sqrt(NY * QUARTER))
    picks = (row == ids).astype(F32).astype(BF16)
    low_ref[...] = (
        jnp.dot(dlogit_t, hp_hi, preferred_element_type=F32)
        + jnp.dot(dlogit_t, hp_lo, preferred_element_type=F32)
        + jnp.dot(picks, ip_hi, preferred_element_type=F32)
        + jnp.dot(picks, ip_lo, preferred_element_type=F32)
    )
    store_low = pltpu.make_async_copy(low_ref, low_hbm, load_sem.at[6])
    store_low.start()

    for copy in started[: -len(third)]:
        copy.wait_send()
    arrive(third)
    grad = in3[0].astype(F32)
    for k in range(1, NZ):
        grad = grad + in3[k].astype(F32)
    grad_ref[...] = unpack(grad).astype(BF16)
    store_low.wait()
    for copy in third:
        copy.wait_send()


def hand_over(loss_in, grad_in, low_in, loss_out, grad_out, low_out):
    low_out[...] = low_in[...]
    grad_out[...] = grad_in[...]
    for i in range(8):
        loss_out[i] = loss_in[i]


def per_device(hidden, table, token_ids, targets, input_grad, projection):
    dma = pltpu.SemaphoreType.DMA
    vmem = pl.BlockSpec(memory_space=pltpu.VMEM)
    smem = pl.BlockSpec(memory_space=pltpu.SMEM)
    hbm = pl.BlockSpec(memory_space=pl.ANY)
    shapes = (
        jax.ShapeDtypeStruct((8,), F32),
        jax.ShapeDtypeStruct((8, SECT), BF16),
        jax.ShapeDtypeStruct((ROWS, RANK), F32),
    )

    def blocks(n, kind=BF16):
        return pltpu.VMEM((n, 2, NX, 16, QUARTER), kind)

    def pairs(*counts):
        return [dma((n,)) for n in counts for _ in range(2)]

    outs = pl.pallas_call(
        kernel,
        out_shape=shapes,
        in_specs=[hbm] * 6,
        out_specs=(smem, vmem, hbm),
        scratch_shapes=[
            pltpu.VMEM((8, SECT), BF16),
            pltpu.SMEM((8,), jnp.int32),
            pltpu.SMEM((8,), jnp.int32),
            pltpu.VMEM((8, SECT), BF16),
            pltpu.VMEM((ROWS, RANK), F32),
            pltpu.VMEM((ROWS, NY * QUARTER), BF16),
            pltpu.VMEM((NY * QUARTER, RANK), BF16),
            pltpu.VMEM((NZ, 16, 384), BF16),
            pltpu.VMEM((NZ, 8, RANK), F32),
            pltpu.VMEM((2, 2, NY, NX, 16, QUARTER), BF16),
            pltpu.VMEM((NY, 2, 16, RANK), BF16),
            pltpu.VMEM((2, NX, 2, 16, RANK), BF16),
            pltpu.VMEM((20, 1, 512), F32),
            pltpu.VMEM((32, 1, 512), F32),
            pltpu.VMEM((ROWS, 256), F32),
            pltpu.VMEM((ROWS, 256), F32),
            pltpu.VMEM((256, ROWS), BF16),
            pltpu.VMEM((2, 2, NX, 16, 128), F32),
            blocks(4),
            blocks(4),
            blocks(4, F32),
            blocks(4),
            blocks(4),
            blocks(4),
            pltpu.VMEM((3, NX, 16, QUARTER), BF16),
            pltpu.VMEM((3, 4, 16, QUARTER), BF16),
            pltpu.VMEM((3, 4, 16, QUARTER), BF16),
            pltpu.VMEM((3, 4, 16, QUARTER), BF16),
            pltpu.VMEM((4, 3, 16, QUARTER), BF16),
            pltpu.VMEM((4, 3, 16, QUARTER), BF16),
            pltpu.VMEM((2, 3, 16, QUARTER), BF16),
            pltpu.VMEM((2, 3, 16, QUARTER), BF16),
            pltpu.VMEM((NZ, 16, 384), BF16),
            pltpu.VMEM((NZ, 16, 384), BF16),
            dma((7,)),
            *pairs(7, 18, 30, 30, 8, 14, 4, 4, 6, 24, 6, 7),
        ],
        compiler_params=pltpu.CompilerParams(
            collective_id=0, has_side_effects=True, vmem_limit_bytes=58 * 2**20
        ),
        cost_estimate=pl.CostEstimate(
            flops=8 * 10**9, bytes_accessed=13 * 10**6, transcendentals=512000
        ),
    )(hidden, table, token_ids, targets, input_grad, projection)
    return pl.pallas_call(
        hand_over,
        out_shape=shapes,
        in_specs=[smem, vmem, vmem],
        out_specs=(smem, vmem, vmem),
    )(*outs)


def solution(mesh):
    placed = (
        P("vocab", "section"),
        P(("vocab", "section"), None),
        P("vocab"),
        P("vocab"),
        P("vocab", "section"),
        P(),
    )
    return jax.shard_map(
        per_device,
        mesh=mesh,
        in_specs=placed,
        out_specs=(P("vocab"), P("vocab", "section"), P(("vocab", "section"), None)),
        check_vma=False,
    )
```
